1024 devices in a mesh: dp: 32 (over y, z_lo), expert: 8 (over x, core), tensor: 4 (over z_hi).
Axes of the slice: x: 4, y: 4, z: 32 (z_hi: 4, z_lo: 8; z = z_hi * 8 + z_lo), core: 2. Of those that a mesh axis runs over, the one named last changes fastest.
Arguments:
- tokens: bfloat16 [512, 6144], P('expert', 'tensor'), may hold values from -6 to 6
- expert_ids: int32 [512, 2], P('expert'), may hold values from 0 to 7, all different within a row; in each aligned block of 64 rows (0 to 63, 64 to 127, ...) at most 32 rows name the same one
- w_gate: bfloat16 [8, 6144, 8192], P('expert', 'tensor', 'dp'), may hold values from -0.078125 to 0.078125
- w_up: bfloat16 [8, 6144, 8192], P('expert', 'tensor', 'dp'), may hold values from -0.078125 to 0.078125
- hidden_grad: bfloat16 [8, 256, 8192], P('expert', None, 'dp'), may hold values from -6 to 6
Outputs:
- tokens_grad: bfloat16 [512, 6144], P('expert', 'tensor')
- gate_grad: bfloat16 [8, 6144, 8192], P('expert', 'tensor', 'dp')
- up_grad: bfloat16 [8, 6144, 8192], P('expert', 'tensor', 'dp')
The draws below stay inside these ranges and needn't reach their ends.
Inputs may be any that keep to these rules, and one draw needn't show every extreme that they name: `expert_ids`: the two ids of a token differ. Within each group of 64 tokens no expert is named by more than 32 tokens.
All inputs are finite; a program needn't handle non-finite values.
Results may differ from the reference program's by a relative error of at most 0.0049.
Values may be sent and summed in bfloat16 or wider, within the bound.
A program may use at most 32 MiB of HBM per device.

```python
import math
import jax
import jax.numpy as jnp
import numpy as np
from jax import lax

D = 6144
FFW = 8192
EXPERTS = 8
TOK_DEV = 64
GROUPS = 8
CAP = 32
ROWS = 256
TOKENS = 512


def block_scale(own_key, shape, split, least, largest):
    factor_of = 1.0
    for dim, shards_of in split:
        draws = jax.random.uniform(jax.random.fold_in(jax.random.fold_in(own_key, 6), dim), (shards_of,), jnp.float32, least / len(split), largest / len(split))
        factor_of = factor_of * jnp.repeat(jnp.exp(draws), shape[dim] // shards_of).reshape((-1,) + (1,) * (len(shape) - 1 - dim))
    return factor_of


def shared_out(rng, own, number, rows, count, top, bound, skew):
    sequence = jax.random.permutation(rng, count)
    packed, ordinary = portions_of(count, rows * top, bound, skew, True), portions_of(count, rows * top, bound, skew, False)
    places = jnp.arange(count)

    def named(tallies, rotation):
        used = int((tallies > 0).sum())
        fixed = max(1, used // 4)
        shifted = fixed + (places - fixed + rotation * (used - fixed)) % max(1, count - fixed)
        return jnp.zeros((count,), jnp.int32).at[sequence[jnp.where(places < fixed, places, shifted)]].set(jnp.asarray(tallies, jnp.int32))

    tallies = jnp.where(number % 4 == 0, named(packed, number // 4), named(ordinary, number - number // 4 - 1))
    mixed = jax.random.permutation(jax.random.fold_in(own, 3), count)
    source_of, sink = mixed[0:count // 2 * 2:2], mixed[1:count // 2 * 2:2]
    slack = jnp.minimum(tallies[source_of] - 1, bound - tallies[sink]) // 2
    slack = jnp.where((source_of == sequence[0]) | (sink == sequence[0]) | (tallies[sink] == 0), 0, jnp.maximum(slack, 0))
    shifted = jax.random.randint(jax.random.fold_in(own, 4), (count // 2,), 0, 1 << 20) % (slack + 1)
    tallies = tallies.at[source_of].add(-shifted).at[sink].add(shifted)
    members = jnp.searchsorted(jnp.cumsum(tallies), jnp.arange(rows * top), side="right").astype(jnp.int32)
    listing = members.reshape(top, rows).T
    listing = listing[jax.random.permutation(jax.random.fold_in(own, 1), rows)]
    rotation = jax.random.randint(jax.random.fold_in(own, 2), (rows, 1), 0, top)
    return jnp.take_along_axis(listing, (jnp.arange(top)[None, :] + rotation) % top, axis=1)


def portions_of(amount, total, bound, slope, full):
    portions = [(1 << 20) // math.isqrt(rank ** slope) + 1 for rank in range(1, amount + 1)]
    largest = bound if full else min(bound, max(-(-total // amount), total * portions[0] // sum(portions)))
    least = 1 if total - largest >= amount - 1 else 0
    counts, surplus = [largest] + [least] * (amount - 1), total - largest - least * (amount - 1)
    while surplus > 0:
        movable = [i for i in range(1, amount) if counts[i] < largest] or [i for i in range(1, amount) if counts[i] < bound]
        whole, budget = sum([portions[i] for i in movable]), surplus
        for i in movable:
            more = min(bound - counts[i], max(1, budget * portions[i] // whole), surplus)
            counts[i] = counts[i] + more
            surplus = surplus - more
    return np.array(counts)


def gaussian(stream_key, shape, spread, most, pieces=(), kind=jnp.bfloat16):
    loudness = block_scale(stream_key, shape, pieces, -0.22, 0.18) if pieces else 1.0
    result = jax.random.normal(stream_key, shape, jnp.float32) * spread * loudness
    return jnp.minimum(jnp.maximum(result, -most), most).astype(kind)


def setup_inputs(seed: int = 0) -> dict:
    key_list = jax.random.split(jax.random.key(seed), 6)
    tokens = gaussian(key_list[0], (TOKENS, D), 1.0, 6.0, ((0, 8), (1, 4)))
    expert_ids_keys = jax.random.split(jax.random.fold_in(key_list[1], 1), TOKENS // TOK_DEV)
    expert_ids_turns = jax.random.permutation(jax.random.fold_in(key_list[1], 3), TOKENS // TOK_DEV)
    expert_ids = jax.vmap(lambda own, number: shared_out(jax.random.fold_in(key_list[1], 2), own, number, TOK_DEV, EXPERTS, 2, CAP, 2))(expert_ids_keys, expert_ids_turns).reshape((TOKENS, 2))
    w_gate = gaussian(key_list[2], (EXPERTS, D, FFW), D ** -0.5, 0.078125, ((0, 8), (1, 4), (2, 32)))
    w_up = gaussian(key_list[3], (EXPERTS, D, FFW), D ** -0.5, 0.078125, ((0, 8), (1, 4), (2, 32)))
    hidden_grad = gaussian(key_list[4], (EXPERTS, ROWS, FFW), 1.0, 6.0, ((0, 8), (2, 32)))
    return dict(tokens=tokens, expert_ids=expert_ids, w_gate=w_gate, w_up=w_up, hidden_grad=hidden_grad)


def slot_tables(expert_ids):
    grouped = expert_ids.reshape(GROUPS, TOK_DEV * 2)
    labels = jnp.arange(EXPERTS, dtype=jnp.int32)
    one_hot = (grouped[:, :, None] == labels[None, None, :]).astype(jnp.int32)
    before = jnp.cumsum(one_hot, axis=1) - one_hot
    slot_rank = jnp.sum(before * one_hot, axis=2)
    target = (grouped * CAP + slot_rank).reshape(GROUPS, TOK_DEV, 2)
    row_index = jnp.arange(EXPERTS * CAP, dtype=jnp.int32)
    hits = (row_index[None, :, None, None] == target[:, None, :, :]).astype(jnp.int32)
    return jnp.sum(hits, axis=3).astype(jnp.float32)


def reference(tokens, expert_ids, w_gate, w_up, hidden_grad):
    tables = slot_tables(expert_ids)
    grouped_tokens = tokens.astype(jnp.float32).reshape(GROUPS, TOK_DEV, D)
    placed = jnp.einsum("spt,std->spd", tables, grouped_tokens, precision=lax.Precision.HIGHEST).astype(jnp.bfloat16)
    expert_rows = placed.reshape(GROUPS, EXPERTS, CAP, D).transpose(1, 0, 2, 3).reshape(EXPERTS, ROWS, D)
    gate_list = []
    up_list = []
    slot_list = []
    for expert in range(EXPERTS):
        rows_here = expert_rows[expert]
        gate_pre = jnp.dot(rows_here, w_gate[expert], preferred_element_type=jnp.float32)
        up_pre = jnp.dot(rows_here, w_up[expert], preferred_element_type=jnp.float32)
        upstream = hidden_grad[expert].astype(jnp.float32)
        sigmoid_gate = jax.nn.sigmoid(gate_pre)
        d_gate = (upstream * up_pre * sigmoid_gate * (1.0 + gate_pre * (1.0 - sigmoid_gate))).astype(jnp.bfloat16)
        d_up = (upstream * gate_pre * sigmoid_gate).astype(jnp.bfloat16)
        dims = (((0,), (0,)), ((), ()))
        gate_list.append(lax.dot_general(rows_here, d_gate, dims, preferred_element_type=jnp.float32).astype(jnp.bfloat16))
        up_list.append(lax.dot_general(rows_here, d_up, dims, preferred_element_type=jnp.float32).astype(jnp.bfloat16))
        back_dims = (((1,), (1,)), ((), ()))
        slot_grad = lax.dot_general(d_gate, w_gate[expert], back_dims, preferred_element_type=jnp.float32)
        slot_grad = slot_grad + lax.dot_general(d_up, w_up[expert], back_dims, preferred_element_type=jnp.float32)
        slot_list.append(slot_grad)
    slot_grads = jnp.stack(slot_list)
    returned = slot_grads.reshape(EXPERTS, GROUPS, CAP, D).transpose(1, 0, 2, 3).reshape(GROUPS, EXPERTS * CAP, D)
    tokens_grad = jnp.einsum("spt,spd->std", tables, returned, precision=lax.Precision.HIGHEST)
    tokens_grad = tokens_grad.reshape(TOKENS, D).astype(jnp.bfloat16)
    return tokens_grad, jnp.stack(gate_list), jnp.stack(up_list)
```

```python
import functools

import jax
import jax.numpy as jnp
from jax import lax
from jax.experimental import pallas as pl
from jax.experimental.pallas import tpu as pltpu
from jax.sharding import PartitionSpec as P

MESH = pl.DeviceIdType.MESH
F32, BF16 = jnp.float32, jnp.bfloat16
ANY = pl.ANY
VMEM = pltpu.VMEM
DMA = pltpu.SemaphoreType.DMA

SLABS = {
    4: ((0, 0), (0, 1), (2, 0), (2, 1), (1, 0), (3, 0), (1, 1), (3, 1)),
    1: ((0, 0), (0, 1)),
}


def remote(src, dst, send, recv, device):
    return pltpu.make_async_remote_copy(
        src_ref=src, dst_ref=dst, send_sem=send, recv_sem=recv, device_id=device, device_id_type=MESH
    )


def kernel(
    sizes,
    ids_ref,
    tok_ref,
    hg_hbm,
    wg_hbm,
    wu_hbm,
    tg_out,
    gg_hbm,
    ug_hbm,
    w_ref,
    hg_ref,
    out_ref,
    x_ref,
    p_ref,
    d_ref,
    r_ref,
    ret_ref,
    s1_snd,
    s1_rcv,
    s2_snd,
    s2_rcv,
    sum_ref,
    ysnd,
    yrcv,
    acc_ref,
    zsnd,
    zrcv,
    og_ref,
    gg_ref,
    ug_ref,
    load_sem,
    store_sem,
    a_send,
    a_recv,
    s1_send,
    s1_recv,
    s2_send,
    s2_recv,
    g1_send,
    g1_recv,
    g2_send,
    g2_recv,
    r_send,
    r_recv,
    y_send,
    y_recv,
    z_send,
    z_recv,
    h_send,
    h_recv,
    o_send,
    o_recv,
):
    ny, nz, nx = sizes
    experts = 2 * nx
    tokens, width = tok_ref.shape
    slots = r_ref.shape[0] // experts
    half = w_ref.shape[1] // 2
    slabs = SLABS[nx]
    chunks = len(slabs) // 2
    rows = 2 * slots
    part = rows // 4

    expert = lax.axis_index("expert")
    core = expert % 2
    x = expert // 2
    dp = lax.axis_index("dp")
    y, zl = dp // nz, dp % nz
    zh = lax.axis_index("tensor")
    up, down = {"tensor": (zh + 1) % 4}, {"tensor": (zh + 3) % 4}

    def place(dx, c):
        return {0: c, 2: 2 + c, 1: 4 + 2 * c, 3: 5 + 2 * c}[dx]

    loads = [
        pltpu.make_async_copy(wg_hbm, w_ref.at[:, pl.ds(0, half)], load_sem.at[0]),
        pltpu.make_async_copy(wu_hbm, w_ref.at[:, pl.ds(half, half)], load_sem.at[1]),
        pltpu.make_async_copy(hg_hbm, hg_ref, load_sem.at[2]),
    ]
    for load in loads:
        load.start()

    barrier = pltpu.get_barrier_semaphore()
    greeted = 0
    for k in range(1, experts):
        pl.semaphore_signal(barrier, 1, device_id={"expert": (expert + k) % experts}, device_id_type=MESH)
        greeted += 1
    for peer in (up, down):
        pl.semaphore_signal(barrier, 1, device_id=peer, device_id_type=MESH)
        greeted += 1
    for k in range(1, ny):
        pl.semaphore_signal(barrier, 1, device_id={"dp": (y + k) % ny * nz + zl}, device_id_type=MESH)
        greeted += 1
    for k in range(1, nz):
        pl.semaphore_signal(barrier, 1, device_id={"dp": y * nz + (zl + k) % nz}, device_id_type=MESH)
        greeted += 1

    total = experts * slots
    lane = lax.broadcasted_iota(jnp.int32, (tokens, total), 1)
    e_of, c_of = lane // slots, lane % slots
    chosen = (ids_ref[:, 0:1] == e_of) | (ids_ref[:, 1:2] == e_of)
    earlier = lax.broadcasted_iota(jnp.int32, (tokens, tokens), 0) > lax.broadcasted_iota(
        jnp.int32, (tokens, tokens), 1
    )
    before = jnp.dot(
        jnp.where(earlier, 1.0, 0.0).astype(BF16),
        jnp.where(chosen, 1.0, 0.0).astype(BF16),
        preferred_element_type=F32,
    )
    table = jnp.where(chosen & (before == c_of.astype(F32)), 1.0, 0.0).astype(BF16)
    out_ref[...] = lax.dot_general(
        table, tok_ref[...], (((0,), (0,)), ((), ())), preferred_element_type=F32
    ).astype(BF16)

    pl.semaphore_wait(barrier, greeted)

    def block(e):
        return pl.ds(pl.multiple_of(e * slots, slots), slots)

    sends = []
    dxs = [0, 1, 3, 2] if nx == 4 else [0]
    flat = 0
    for dx in dxs:
        for c in range(2):
            if dx == 0 and c == 1:
                continue
            other = 1 - core if dx == 0 else c
            to = ((x + nx - dx) % nx) * 2 + other
            slab = place(dx, core)
            copy = remote(
                out_ref.at[block(to)], x_ref.at[block(slab)], a_send.at[flat], a_recv.at[slab], {"expert": to}
            )
            copy.start()
            sends.append(copy)
            flat += 1
    x_ref[block(core), :] = out_ref[block(expert), :]

    def source(p):
        dx, c = slabs[p]
        return ((x + dx) % nx) * 2 + c

    def wait_slabs(j):
        for p in (2 * j, 2 * j + 1):
            if slabs[p][0] == 0:
                if p == 0:
                    q = 1 - core
                    remote(
                        out_ref.at[block(0)], x_ref.at[block(q)], a_send.at[0], a_recv.at[q], {"expert": expert}
                    ).wait_recv()
            else:
                remote(
                    out_ref.at[block(0)], x_ref.at[block(p)], a_send.at[0], a_recv.at[p], {"expert": expert}
                ).wait_recv()

    def piece(j, k):
        return pl.ds(pl.multiple_of(j * rows + k * part, part), part)

    lo, hi = pl.ds(0, half), pl.ds(half, half)
    dirs = ((up, lo), (down, hi))

    def s1(j, d):
        return remote(s1_snd.at[j, d], s1_rcv.at[j, d], s1_send.at[j, d], s1_recv.at[j, d], dirs[d][0])

    def s2(j, d):
        return remote(s2_snd.at[j, d], s2_rcv.at[j, d], s2_send.at[j, d], s2_recv.at[j, d], dirs[d][0])

    def g1(j, d):
        ref = d_ref.at[piece(j, zh)]
        return remote(ref, ref, g1_send.at[j, d], g1_recv.at[j, d], dirs[d][0])

    def g2(j, d):
        ref = d_ref.at[piece(j, (zh + (3 if d == 0 else 1)) % 4), dirs[d][1]]
        return remote(ref, ref, g2_send.at[j, d], g2_recv.at[j, d], dirs[d][0])

    def stage0(j):
        wait_slabs(j)
        if j == 0:
            loads[0].wait()
            loads[1].wait()
        own = pl.ds(j * rows, rows)
        p_ref[own, :] = jnp.dot(x_ref[own, :], w_ref[...], preferred_element_type=F32)
        far = piece(j, (zh + 2) % 4)
        s1_snd[j, 0] = p_ref[far, lo].astype(BF16)
        s1_snd[j, 1] = p_ref[far, hi].astype(BF16)
        for d in range(2):
            s1(j, d).start()
            sends.append(s1(j, d))

    def stage1(j):
        for d in range(2):
            to = piece(j, (zh + (1 if d == 0 else 3)) % 4)
            mixed, plain = (lo, hi) if d == 0 else (hi, lo)
            s2_snd[j, d, :, plain] = p_ref[to, plain].astype(BF16)
            s1(j, d).wait_recv()
            s2_snd[j, d, :, mixed] = (p_ref[to, mixed] + s1_rcv[j, d].astype(F32)).astype(BF16)
            s2(j, d).start()
            sends.append(s2(j, d))

    def stage2(j):
        if j == 0:
            loads[2].wait()
        mine = piece(j, zh)
        group = jnp.where(zh < 2, source(2 * j), source(2 * j + 1))
        hg_rows = pl.ds(pl.multiple_of(group * slots + zh % 2 * part, part), part)
        upstream = hg_ref[hg_rows, :].astype(F32)
        for d in range(2):
            s2(j, d).wait_recv()
        gate = p_ref[mine, lo] + s2_rcv[j, 0, :, lo].astype(F32) + s2_rcv[j, 1, :, lo].astype(F32)
        upp = p_ref[mine, hi] + s2_rcv[j, 0, :, hi].astype(F32) + s2_rcv[j, 1, :, hi].astype(F32)
        sg = jax.nn.sigmoid(gate)
        d_ref[mine, lo] = (upstream * upp * sg * (1.0 + gate * (1.0 - sg))).astype(BF16)
        d_ref[mine, hi] = (upstream * gate * sg).astype(BF16)
        for d in range(2):
            g1(j, d).start()
            sends.append(g1(j, d))

    def got1(j, d):
        ref = d_ref.at[piece(j, (zh + (3 if d == 0 else 1)) % 4)]
        return remote(ref, ref, g1_send.at[j, d], g1_recv.at[j, d], dirs[d][0])

    def got2(j, d):
        ref = d_ref.at[piece(j, (zh + 2) % 4), dirs[d][1]]
        return remote(ref, ref, g2_send.at[j, d], g2_recv.at[j, d], dirs[d][0])

    def stage3(j):
        for d in range(2):
            got1(j, d).wait_recv()
            g2(j, d).start()
            sends.append(g2(j, d))

    def stage4(j):
        for d in range(2):
            got2(j, d).wait_recv()
        own = pl.ds(j * rows, rows)
        r_ref[own, :] = lax.dot_general(
            d_ref[own, :], w_ref[...], (((1,), (1,)), ((), ())), preferred_element_type=F32
        ).astype(BF16)
        for p in (2 * j, 2 * j + 1):
            dx, c = slabs[p]
            if dx == 0:
                if p % 2:
                    continue
                p, to = 1 - core, x * 2 + 1 - core
            else:
                to = source(p)
            index = place((nx - dx) % nx, core)
            copy = remote(
                r_ref.at[block(p)], ret_ref.at[block(expert)], r_send.at[p], r_recv.at[index], {"expert": to}
            )
            copy.start()
            sends.append(copy)
        if j == 0:
            ret_ref[block(expert), :] = r_ref[block(core), :]

    stages = (stage0, stage1, stage2, stage3, stage4)
    for t in range(chunks + len(stages) - 1):
        for s in reversed(range(len(stages))):
            if 0 <= t - s < chunks:
                stages[s](t - s)

    step = min(256, width)

    def grads(i, carry):
        cols = pl.ds(pl.multiple_of(i * step, step), step)
        both = lax.dot_general(
            x_ref[:, cols], d_ref[...], (((0,), (0,)), ((), ())), preferred_element_type=F32
        ).astype(BF16)
        gg_ref[cols, :] = both[:, :half]
        ug_ref[cols, :] = both[:, half:]
        return carry

    lax.fori_loop(0, width // step, grads, 0)
    stores = [
        pltpu.make_async_copy(gg_ref, gg_hbm, store_sem.at[0]),
        pltpu.make_async_copy(ug_ref, ug_hbm, store_sem.at[1]),
    ]
    for store in stores:
        store.start()

    for p in range(len(slabs)):
        dx, c = slabs[p]
        if dx == 0:
            if p:
                continue
            index, e = 1 - core, x * 2 + 1 - core
        else:
            index, e = p, source(p)
        remote(
            r_ref.at[block(0)], ret_ref.at[block(e)], r_send.at[0], r_recv.at[index], {"expert": expert}
        ).wait_recv()
    sum_ref[...] = jnp.dot(table, ret_ref[...], preferred_element_type=F32)

    share = tokens // ny

    def band(k):
        return pl.ds(pl.multiple_of(k * share, share), share)

    mine = band(y)
    acc = sum_ref[mine, :]
    if ny > 1:
        ysnd[...] = sum_ref[...].astype(BF16)
        for k in range(1, ny):
            to = (y + k) % ny
            copy = remote(
                ysnd.at[band(to)], yrcv.at[k - 1], y_send.at[k - 1], y_recv.at[k - 1], {"dp": to * nz + zl}
            )
            copy.start()
            sends.append(copy)
        for k in range(1, ny):
            remote(
                ysnd.at[band(0)], yrcv.at[k - 1], y_send.at[k - 1], y_recv.at[k - 1], {"dp": dp}
            ).wait_recv()
            acc = acc + yrcv[k - 1].astype(F32)
    acc_ref[...] = acc

    owners = min(4, nz)
    first = (nz - owners) // 2
    wide = width // owners
    zsnd[...] = acc.astype(BF16)

    def z_out(m):
        rel = (zl + nz - (first + m)) % nz
        return remote(
            zsnd.at[:, pl.ds(m * wide, wide)],
            zrcv.at[rel],
            z_send.at[m],
            z_recv.at[rel],
            {"dp": y * nz + first + m},
        )

    is_owner = (zl >= first) & (zl < first + owners)
    my_cols = pl.ds(pl.multiple_of(jnp.clip(zl - first, 0, owners - 1) * wide, 128), wide)
    my_m = jnp.clip(zl - first, 0, owners - 1)

    def h_out(k):
        ref = og_ref.at[mine, my_cols]
        return remote(ref, ref, h_send.at[k], h_recv.at[my_m], {"dp": y * nz + (zl + k) % nz})

    for m in range(owners):
        pl.when(zl != first + m)(lambda m=m: z_out(m).start())

    @pl.when(is_owner)
    def _():
        value = acc_ref[:, my_cols]
        for k in range(1, nz):
            remote(
                zsnd.at[:, pl.ds(0, wide)], zrcv.at[k], z_send.at[0], z_recv.at[k], {"dp": dp}
            ).wait_recv()
            value = value + zrcv[k].astype(F32)
        og_ref[mine, my_cols] = value.astype(BF16)
        for k in range(1, nz):
            h_out(k).start()

    for m in range(owners):

        @pl.when(zl != first + m)
        def _(m=m):
            ref = og_ref.at[mine, pl.ds(m * wide, wide)]
            remote(ref, ref, h_send.at[0], h_recv.at[m], {"dp": dp}).wait_recv()

    for k in range(1, ny):
        ref = og_ref.at[mine]
        copy = remote(ref, ref, o_send.at[k - 1], o_recv.at[k - 1], {"dp": (y + k) % ny * nz + zl})
        copy.start()
        sends.append(copy)
    for k in range(1, ny):
        ref = og_ref.at[band((y + ny - k) % ny)]
        remote(ref, ref, o_send.at[k - 1], o_recv.at[k - 1], {"dp": dp}).wait_recv()
    tg_out[...] = og_ref[...]

    for copy in sends:
        copy.wait_send()
    for m in range(owners):
        pl.when(zl != first + m)(lambda m=m: z_out(m).wait_send())

    @pl.when(is_owner)
    def _():
        for k in range(1, nz):
            h_out(k).wait_send()

    for store in stores:
        store.wait()


def on_device(sizes, tokens, expert_ids, w_gate, w_up, hidden_grad):
    ny, nz, nx = sizes
    count, width = tokens.shape
    half = w_gate.shape[2]
    rows = hidden_grad.shape[1]
    chunks = nx
    part = rows // chunks // 4
    share = count // ny
    owners = min(4, nz)
    near = max(ny - 1, 1)
    scratch = [
        VMEM((width, 2 * half), BF16),
        VMEM((rows, half), BF16),
        VMEM((rows, width), BF16),
        VMEM((rows, width), BF16),
        VMEM((rows, 2 * half), F32),
        VMEM((rows, 2 * half), BF16),
        VMEM((rows, width), BF16),
        VMEM((rows, width), BF16),
        VMEM((chunks, 2, part, half), BF16),
        VMEM((chunks, 2, part, half), BF16),
        VMEM((chunks, 2, part, 2 * half), BF16),
        VMEM((chunks, 2, part, 2 * half), BF16),
        VMEM((count, width), F32),
        VMEM((count, width), BF16),
        VMEM((near, share, width), BF16),
        VMEM((share, width), F32),
        VMEM((share, width), BF16),
        VMEM((nz, share, width // owners), BF16),
        VMEM((count, width), BF16),
        VMEM((width, half), BF16),
        VMEM((width, half), BF16),
        DMA((3,)),
        DMA((2,)),
        DMA((2 * nx,)),
        DMA((2 * nx,)),
    ]
    scratch += [DMA((chunks, 2)) for _ in range(8)]
    scratch += [
        DMA((2 * nx,)),
        DMA((2 * nx,)),
        DMA((near,)),
        DMA((near,)),
        DMA((owners,)),
        DMA((nz,)),
        DMA((nz,)),
        DMA((owners,)),
        DMA((near,)),
        DMA((near,)),
    ]
    vmem = pl.BlockSpec(memory_space=VMEM)
    hbm = pl.BlockSpec(memory_space=ANY)
    tokens_grad, gate_grad, up_grad = pl.pallas_call(
        functools.partial(kernel, sizes),
        out_shape=(
            jax.ShapeDtypeStruct((count, width), BF16),
            jax.ShapeDtypeStruct((width, half), BF16),
            jax.ShapeDtypeStruct((width, half), BF16),
        ),
        in_specs=[vmem, vmem, hbm, hbm, hbm],
        out_specs=(vmem, hbm, hbm),
        scratch_shapes=scratch,
        compiler_params=pltpu.CompilerParams(
            collective_id=0, has_side_effects=True, vmem_limit_bytes=40 * 1024 * 1024
        ),
    )(expert_ids, tokens, hidden_grad[0], w_gate[0], w_up[0])
    return tokens_grad, gate_grad[None], up_grad[None]


def solution(mesh):
    dp, experts = mesh.shape["dp"], mesh.shape["expert"]
    sizes = {32: (4, 8), 4: (2, 2), 1: (1, 1)}[dp] + (experts // 2,)
    in_specs = (
        P("expert", "tensor"),
        P("expert", None),
        P("expert", "tensor", "dp"),
        P("expert", "tensor", "dp"),
        P("expert", None, "dp"),
    )
    out_specs = (P("expert", "tensor"), P("expert", "tensor", "dp"), P("expert", "tensor", "dp"))
    return jax.shard_map(
        functools.partial(on_device, sizes),
        mesh=mesh,
        in_specs=in_specs,
        out_specs=out_specs,
        check_vma=False,
    )
```

```python
import functools

import jax
import jax.numpy as jnp
from jax import lax
from jax.experimental import pallas as pl
from jax.experimental.pallas import tpu as pltpu
from jax.sharding import PartitionSpec as P

MESH = pl.DeviceIdType.MESH
F32, BF16 = jnp.float32, jnp.bfloat16
ANY = pl.ANY
VMEM = pltpu.VMEM
DMA = pltpu.SemaphoreType.DMA

SLABS = {
    4: ((0, 0), (0, 1), (1, 0), (3, 1), (2, 0), (2, 1), (1, 1), (3, 0)),
    1: ((0, 0), (0, 1)),
}


def remote(src, dst, send, recv, device):
    return pltpu.make_async_remote_copy(
        src_ref=src, dst_ref=dst, send_sem=send, recv_sem=recv, device_id=device, device_id_type=MESH
    )


def kernel(
    sizes,
    ids_ref,
    tok_ref,
    hg_hbm,
    wg_hbm,
    wu_hbm,
    tg_out,
    gg_hbm,
    ug_hbm,
    table_ref,
    w_ref,
    hg_ref,
    out_ref,
    x_ref,
    p_ref,
    d_ref,
    r_ref,
    rf_ref,
    yrcv,
    ysum,
    ret_ref,
    s1_snd,
    s1_rcv,
    s2_snd,
    s2_rcv,
    sum_ref,
    zsnd,
    zrcv,
    og_ref,
    gg_ref,
    ug_ref,
    load_sem,
    store_sem,
    a_send,
    a_recv,
    f_send,
    f_recv,
    s1_send,
    s1_recv,
    s2_send,
    s2_recv,
    g1_send,
    g1_recv,
    r_send,
    r_recv,
    y_send,
    y_recv,
    z_send,
    z_recv,
    h_send,
    h_recv,
    o_send,
    o_recv,
):
    ny, nz, nx = sizes
    experts = 2 * nx
    tokens, width = tok_ref.shape
    slots = r_ref.shape[0] // experts
    half = w_ref.shape[1] // 2
    slabs = SLABS[nx]
    cuts = z_send.shape[1]
    share = width // ny
    span = share // cuts
    chunks = len(slabs) // 2
    rows = 2 * slots
    part = rows // 4

    expert = lax.axis_index("expert")
    core = expert % 2
    x = expert // 2
    dp = lax.axis_index("dp")
    y, zl = dp // nz, dp % nz
    zh = lax.axis_index("tensor")
    pair = ({"tensor": zh + 1 - 2 * (zh % 2)}, {"tensor": 3 - zh})
    kept = ((zh + 1) % 4 // 2, zh // 2)

    def place(dx, c):
        return {0: c, 1: 2 + 4 * c, 2: 4 + c, 3: 7 - 4 * c}[dx]

    def cols_of(k):
        return pl.ds(pl.multiple_of(k * share, 128), share)

    def cut_of(k, q):
        return pl.ds(pl.multiple_of(k * share + q * span, 128), span)

    barrier = pltpu.get_barrier_semaphore()
    greeted = 0
    for peer in pair:
        pl.semaphore_signal(barrier, 1, device_id=peer, device_id_type=MESH)
        greeted += 1
    for k in range(1, experts):
        pl.semaphore_signal(barrier, 1, device_id={"expert": (expert + k) % experts}, device_id_type=MESH)
        greeted += 1
    for k in range(1, ny):
        pl.semaphore_signal(barrier, 1, device_id={"dp": (y + k) % ny * nz + zl}, device_id_type=MESH)
        greeted += 1
    for k in range(1, nz):
        pl.semaphore_signal(barrier, 1, device_id={"dp": y * nz + (zl + k) % nz}, device_id_type=MESH)
        greeted += 1

    loads = [
        pltpu.make_async_copy(wg_hbm, w_ref.at[:, pl.ds(0, half)], load_sem.at[0]),
        pltpu.make_async_copy(wu_hbm, w_ref.at[:, pl.ds(half, half)], load_sem.at[1]),
        pltpu.make_async_copy(hg_hbm, hg_ref, load_sem.at[2]),
    ]
    for load in loads:
        load.start()

    total = experts * slots
    row = lax.broadcasted_iota(jnp.int32, (total, tokens), 0)
    chosen = (ids_ref[0:1, :] == row // slots) | (ids_ref[1:2, :] == row // slots)
    earlier = lax.broadcasted_iota(jnp.int32, (tokens, tokens), 0) < lax.broadcasted_iota(
        jnp.int32, (tokens, tokens), 1
    )
    before = jnp.dot(
        jnp.where(chosen, 1.0, 0.0).astype(BF16),
        jnp.where(earlier, 1.0, 0.0).astype(BF16),
        preferred_element_type=F32,
    )
    table = jnp.where(chosen & (before == (row % slots).astype(F32)), 1.0, 0.0)
    table_ref[...] = table.T.astype(BF16)
    out_ref[...] = jnp.dot(table.astype(BF16), tok_ref[...], preferred_element_type=F32).astype(BF16)

    pl.semaphore_wait(barrier, greeted)

    def block(e):
        return pl.ds(pl.multiple_of(e * slots, slots), slots)

    sends = []
    dxs = [0, 2, 1, 3] if nx == 4 else [0]
    flat = 0
    for dx in dxs:
        for c in range(2):
            if dx == 0 and c == 1:
                continue
            other = 1 - core if dx == 0 else c
            to = ((x + nx - dx) % nx) * 2 + other
            slab = place(dx, core)
            src, dst = out_ref.at[block(to)], x_ref.at[block(slab)]
            if dx == 2:
                src, dst = out_ref.at[block(to), cols_of(y)], x_ref.at[block(slab), cols_of(y)]
            copy = remote(src, dst, a_send.at[flat], a_recv.at[slab], {"expert": to})
            copy.start()
            sends.append(copy)
            flat += 1
    x_ref[block(core), :] = out_ref[block(expert), :]

    def source(p):
        dx, c = slabs[p]
        return ((x + dx) % nx) * 2 + c

    def wait_slabs(j):
        for p in (2 * j, 2 * j + 1):
            if slabs[p][0] == 0:
                if p == 0:
                    q = 1 - core
                    remote(
                        out_ref.at[block(0)], x_ref.at[block(q)], a_send.at[0], a_recv.at[q], {"expert": expert}
                    ).wait_recv()
            elif slabs[p][0] != 2:
                remote(
                    out_ref.at[block(0)], x_ref.at[block(p)], a_send.at[0], a_recv.at[p], {"expert": expert}
                ).wait_recv()
            elif p % 2 == 0:
                for k in range(1, ny):
                    spread(k, y + ny - k).wait_recv()

    far_rows = pl.ds(2 * rows, rows)

    def spread(k, owner):
        ref = x_ref.at[far_rows, cols_of(owner % ny)]
        return remote(ref, ref, f_send.at[k - 1], f_recv.at[k - 1], {"dp": (y + k) % ny * nz + zl})

    def hand_on():
        for p in (4, 5):
            remote(
                out_ref.at[block(0), cols_of(y)],
                x_ref.at[block(p), cols_of(y)],
                a_send.at[0],
                a_recv.at[p],
                {"expert": expert},
            ).wait_recv()
        for k in range(1, ny):
            spread(k, y).start()
            sends.append(spread(k, y))

    def piece(j, d, h):
        return pl.ds(pl.multiple_of(j * rows + d * slots + h * part, part), part)

    lo, hi = pl.ds(0, half), pl.ds(half, half)

    def s1(j, d):
        return remote(s1_snd.at[j, d], s1_rcv.at[j, d], s1_send.at[j, d], s1_recv.at[j, d], pair[d])

    def s2(j, d):
        return remote(s2_snd.at[j, d], s2_rcv.at[j, d], s2_send.at[j, d], s2_recv.at[j, d], pair[1 - d])

    def g1(j, d, h):
        ref = d_ref.at[piece(j, d, h)]
        return remote(ref, ref, g1_send.at[j, d], g1_recv.at[j, d], pair[d])

    def stage0(j):
        wait_slabs(j)
        if j == 0:
            loads[0].wait()
            loads[1].wait()
        own = pl.ds(j * rows, rows)
        p_ref[own, :] = jnp.dot(x_ref[own, :], w_ref[...], preferred_element_type=F32)
        for d in range(2):
            s1_snd[j, d] = p_ref[piece(j, d, 1 - kept[d]), :].astype(BF16)
        for d in range(2):
            s1(j, d).start()
            sends.append(s1(j, d))

    def stage1(j):
        for d in range(2):
            mine = piece(j, d, kept[d])
            s1(j, d).wait_recv()
            both = p_ref[mine, :] + s1_rcv[j, d].astype(F32)
            p_ref[mine, :] = both
            s2_snd[j, d] = both.astype(BF16)
            s2(j, d).start()
            sends.append(s2(j, d))

    def stage2(j):
        if j == 0:
            loads[2].wait()
        for d in range(2):
            mine = piece(j, d, kept[d])
            hg_rows = pl.ds(pl.multiple_of(source(2 * j + d) * slots + kept[d] * part, part), part)
            upstream = hg_ref[hg_rows, :].astype(F32)
            s2(j, d).wait_recv()
            gate = p_ref[mine, lo] + s2_rcv[j, d, :, lo].astype(F32)
            upp = p_ref[mine, hi] + s2_rcv[j, d, :, hi].astype(F32)
            sg = jax.nn.sigmoid(gate)
            d_ref[mine, lo] = (upstream * upp * sg * (1.0 + gate * (1.0 - sg))).astype(BF16)
            d_ref[mine, hi] = (upstream * gate * sg).astype(BF16)
            g1(j, d, kept[d]).start()
            sends.append(g1(j, d, kept[d]))

    def stage4(j):
        for d in range(2):
            g1(j, d, 1 - kept[d]).wait_recv()
        own = pl.ds(j * rows, rows)
        rf_ref[own, :] = lax.dot_general(
            d_ref[own, :], w_ref[...], (((1,), (1,)), ((), ())), preferred_element_type=F32
        )
        r_ref[own, :] = rf_ref[own, :].astype(BF16)
        for k in range(1, ny):
            to = (y + k) % ny
            copy = remote(
                r_ref.at[own, cols_of(to)],
                yrcv.at[j, k - 1],
                y_send.at[j, k - 1],
                y_recv.at[j, k - 1],
                {"dp": to * nz + zl},
            )
            copy.start()
            sends.append(copy)

    def stage5(j):
        own = pl.ds(j * rows, rows)
        value = rf_ref[own, cols_of(y)]
        for k in range(1, ny):
            ref = yrcv.at[j, k - 1]
            remote(ref, ref, y_send.at[j, k - 1], y_recv.at[j, k - 1], {"dp": dp}).wait_recv()
            value = value + yrcv[j, k - 1].astype(F32)
        ysum[own, :] = value.astype(BF16)
        for p in (2 * j, 2 * j + 1):
            dx, c = slabs[p]
            if dx == 0:
                if p % 2:
                    continue
                p, to = 1 - core, x * 2 + 1 - core
            else:
                to = source(p)
            index = place((nx - dx) % nx, core)
            copy = remote(
                ysum.at[block(p)], ret_ref.at[block(expert)], r_send.at[p], r_recv.at[index], {"expert": to}
            )
            copy.start()
            sends.append(copy)
        if j == 0:
            ret_ref[block(expert), :] = ysum[block(core), :]

    if nx == 4:
        plan = (0, 0), (0, 1), "F", (0, 3), (1, 0), (0, 2), (1, 1), (1, 3), (1, 2), (2, 0), (2, 1), (2, 2), (2, 3), (4, 0), (4, 1), (4, 2), (5, 0), (5, 1), (4, 3), "V", (5, 2), (5, 3), "W"
    else:
        plan = (0, 0), (1, 0), (2, 0), (4, 0), "V", (5, 0), "W"
    step = min(256, width)
    early = width // step // 2

    def grads(i, carry):
        cols = pl.ds(pl.multiple_of(i * step, step), step)
        both = lax.dot_general(
            x_ref[:, cols], d_ref[...], (((0,), (0,)), ((), ())), preferred_element_type=F32
        ).astype(BF16)
        gg_ref[cols, :] = both[:, :half]
        ug_ref[cols, :] = both[:, half:]
        return carry

    stores = [
        pltpu.make_async_copy(gg_ref, gg_hbm, store_sem.at[0]),
        pltpu.make_async_copy(ug_ref, ug_hbm, store_sem.at[1]),
    ]
    stages = (stage0, stage1, stage2, None, stage4, stage5)
    for act in plan:
        if act == "F":
            hand_on()
        elif act == "V":
            lax.fori_loop(0, early, grads, 0)
        elif act == "W":
            lax.fori_loop(early, width // step, grads, 0)
            for store in stores:
                store.start()
        else:
            stages[act[0]](act[1])

    for p in range(len(slabs)):
        dx, c = slabs[p]
        if dx == 0:
            if p:
                continue
            index, e = 1 - core, x * 2 + 1 - core
        else:
            index, e = p, source(p)
        ref = ret_ref.at[block(e)]
        remote(ref, ref, r_send.at[0], r_recv.at[index], {"expert": expert}).wait_recv()
    sum_ref[...] = jnp.dot(table_ref[...], ret_ref[...], preferred_element_type=F32)
    zsnd[...] = sum_ref[...].astype(BF16)

    owners = z_send.shape[0]
    first = (nz - owners) // 2
    few = tokens // owners
    is_owner = (zl >= first) & (zl < first + owners)
    my_m = jnp.clip(zl - first, 0, owners - 1)

    def band(m):
        return pl.ds(pl.multiple_of(m * few, few), few)

    def z_out(q, m):
        rel = (zl + nz - (first + m)) % nz
        return remote(
            zsnd.at[band(m), pl.ds(q * span, span)],
            zrcv.at[rel, :, pl.ds(q * span, span)],
            z_send.at[m, q],
            z_recv.at[rel, q],
            {"dp": y * nz + first + m},
        )

    def h_out(q, k):
        ref = og_ref.at[band(my_m), cut_of(y, q)]
        return remote(ref, ref, h_send.at[k, q], h_recv.at[my_m, q], {"dp": y * nz + (zl + k) % nz})

    for q in range(cuts):
        for m in range(owners):
            pl.when(zl != first + m)(lambda q=q, m=m: z_out(q, m).start())

    @pl.when(is_owner)
    def _():
        for q in range(cuts):
            value = sum_ref[band(my_m), pl.ds(q * span, span)]
            for k in range(1, nz):
                ref = zrcv.at[k, :, pl.ds(q * span, span)]
                remote(ref, ref, z_send.at[0, q], z_recv.at[k, q], {"dp": dp}).wait_recv()
                value = value + zrcv[k, :, pl.ds(q * span, span)].astype(F32)
            og_ref[band(my_m), cut_of(y, q)] = value.astype(BF16)
            for k in range(1, nz):
                h_out(q, k).start()

    for q in range(cuts):
        for m in range(owners):

            @pl.when(zl != first + m)
            def _(q=q, m=m):
                ref = og_ref.at[band(m), cut_of(y, q)]
                remote(ref, ref, h_send.at[0, q], h_recv.at[m, q], {"dp": dp}).wait_recv()

        for k in range(1, ny):
            ref = og_ref.at[:, cut_of(y, q)]
            copy = remote(ref, ref, o_send.at[k - 1, q], o_recv.at[k - 1, q], {"dp": (y + k) % ny * nz + zl})
            copy.start()
            sends.append(copy)
    for q in range(cuts):
        for k in range(1, ny):
            ref = og_ref.at[:, cut_of((y + ny - k) % ny, q)]
            remote(ref, ref, o_send.at[k - 1, q], o_recv.at[k - 1, q], {"dp": dp}).wait_recv()
    tg_out[...] = og_ref[...]

    for copy in sends:
        copy.wait_send()
    for q in range(cuts):
        for m in range(owners):
            pl.when(zl != first + m)(lambda q=q, m=m: z_out(q, m).wait_send())

    @pl.when(is_owner)
    def _():
        for q in range(cuts):
            for k in range(1, nz):
                h_out(q, k).wait_send()

    for store in stores:
        store.wait()


def on_device(sizes, tokens, expert_ids, w_gate, w_up, hidden_grad):
    ny, nz, nx = sizes
    count, width = tokens.shape
    half = w_gate.shape[2]
    rows = hidden_grad.shape[1]
    chunks = nx
    part = rows // chunks // 4
    share = width // ny
    owners = min(4, nz)
    near = max(ny - 1, 1)
    cuts = 1
    scratch = [
        VMEM((count, rows), BF16),
        VMEM((width, 2 * half), BF16),
        VMEM((rows, half), BF16),
        VMEM((rows, width), BF16),
        VMEM((rows, width), BF16),
        VMEM((rows, 2 * half), F32),
        VMEM((rows, 2 * half), BF16),
        VMEM((rows, width), BF16),
        VMEM((rows, width), F32),
        VMEM((chunks, near, rows // chunks, share), BF16),
        VMEM((rows, share), BF16),
        VMEM((rows, share), BF16),
        VMEM((chunks, 2, part, 2 * half), BF16),
        VMEM((chunks, 2, part, 2 * half), BF16),
        VMEM((chunks, 2, part, 2 * half), BF16),
        VMEM((chunks, 2, part, 2 * half), BF16),
        VMEM((count, share), F32),
        VMEM((count, share), BF16),
        VMEM((nz, count // owners, share), BF16),
        VMEM((count, width), BF16),
        VMEM((width, half), BF16),
        VMEM((width, half), BF16),
        DMA((3,)),
        DMA((2,)),
        DMA((2 * nx,)),
        DMA((2 * nx,)),
        DMA((near,)),
        DMA((near,)),
    ]
    scratch += [DMA((chunks, 2)) for _ in range(6)]
    scratch += [
        DMA((2 * nx,)),
        DMA((2 * nx,)),
        DMA((chunks, near)),
        DMA((chunks, near)),
        DMA((owners, cuts)),
        DMA((nz, cuts)),
        DMA((nz, cuts)),
        DMA((owners, cuts)),
        DMA((near, cuts)),
        DMA((near, cuts)),
    ]
    vmem = pl.BlockSpec(memory_space=VMEM)
    hbm = pl.BlockSpec(memory_space=ANY)
    tokens_grad, gate_grad, up_grad = pl.pallas_call(
        functools.partial(kernel, sizes),
        out_shape=(
            jax.ShapeDtypeStruct((count, width), BF16),
            jax.ShapeDtypeStruct((width, half), BF16),
            jax.ShapeDtypeStruct((width, half), BF16),
        ),
        in_specs=[vmem, vmem, hbm, hbm, hbm],
        out_specs=(vmem, hbm, hbm),
        scratch_shapes=scratch,
        compiler_params=pltpu.CompilerParams(
            collective_id=0, has_side_effects=True, vmem_limit_bytes=60 * 1024 * 1024
        ),
    )(expert_ids.T, tokens, hidden_grad[0], w_gate[0], w_up[0])
    return tokens_grad, gate_grad[None], up_grad[None]


def solution(mesh):
    dp, experts = mesh.shape["dp"], mesh.shape["expert"]
    sizes = {32: (4, 8), 4: (2, 2), 2: (2, 1), 1: (1, 1)}[dp] + (experts // 2,)
    in_specs = (
        P("expert", "tensor"),
        P("expert", None),
        P("expert", "tensor", "dp"),
        P("expert", "tensor", "dp"),
        P("expert", None, "dp"),
    )
    out_specs = (P("expert", "tensor"), P("expert", "tensor", "dp"), P("expert", "tensor", "dp"))
    return jax.shard_map(
        functools.partial(on_device, sizes),
        mesh=mesh,
        in_specs=in_specs,
        out_specs=out_specs,
        check_vma=False,
    )
```

```python
import functools

import jax
import jax.numpy as jnp
from jax import lax
from jax.experimental import pallas as pl
from jax.experimental.pallas import tpu as pltpu
from jax.sharding import PartitionSpec as P

MESH = pl.DeviceIdType.MESH
F32, BF16 = jnp.float32, jnp.bfloat16
ANY = pl.ANY
VMEM = pltpu.VMEM
DMA = pltpu.SemaphoreType.DMA

SLABS = {
    4: ((0, 0), (0, 1), (1, 0), (3, 1), (2, 0), (2, 1), (1, 1), (3, 0)),
    1: ((0, 0), (0, 1)),
}


def remote(src, dst, send, recv, device):
    return pltpu.make_async_remote_copy(
        src_ref=src, dst_ref=dst, send_sem=send, recv_sem=recv, device_id=device, device_id_type=MESH
    )


def kernel(
    sizes,
    ids_ref,
    tok_hbm,
    hg_hbm,
    wg_hbm,
    wu_hbm,
    tg_out,
    gg_hbm,
    ug_hbm,
    tok_ref,
    table_ref,
    w_ref,
    hg_ref,
    out_ref,
    x_ref,
    p_ref,
    d_ref,
    r_ref,
    rf_ref,
    yrcv,
    ysum,
    ret_ref,
    s1_snd,
    s1_rcv,
    s2_snd,
    s2_rcv,
    sum_ref,
    zsnd,
    zrcv,
    og_ref,
    gg_ref,
    ug_ref,
    load_sem,
    store_sem,
    a_send,
    a_recv,
    f_send,
    f_recv,
    s1_send,
    s1_recv,
    s2_send,
    s2_recv,
    g1_send,
    g1_recv,
    r_send,
    r_recv,
    y_send,
    y_recv,
    z_send,
    z_recv,
    h_send,
    h_recv,
    o_send,
    o_recv,
):
    ny, nz, nx = sizes
    experts = 2 * nx
    tokens, width = tok_ref.shape
    slots = r_ref.shape[0] // experts
    half = w_ref.shape[1] // 2
    slabs = SLABS[nx]
    cuts = z_send.shape[1]
    share = width // ny
    span = share // cuts
    chunks = len(slabs) // 2
    rows = 2 * slots
    part = rows // 4

    expert = lax.axis_index("expert")
    core = expert % 2
    x = expert // 2
    dp = lax.axis_index("dp")
    y, zl = dp // nz, dp % nz
    zh = lax.axis_index("tensor")
    pair = ({"tensor": zh + 1 - 2 * (zh % 2)}, {"tensor": 3 - zh})
    kept = ((zh + 1) % 4 // 2, zh // 2)

    def place(dx, c):
        return {0: c, 1: 2 + 4 * c, 2: 4 + c, 3: 7 - 4 * c}[dx]

    def cols_of(k):
        return pl.ds(pl.multiple_of(k * share, 128), share)

    def cut_of(k, q):
        return pl.ds(pl.multiple_of(k * share + q * span, 128), span)

    barrier = pltpu.get_barrier_semaphore()
    greeted = 0
    for peer in pair:
        pl.semaphore_signal(barrier, 1, device_id=peer, device_id_type=MESH)
        greeted += 1
    for k in range(1, experts):
        pl.semaphore_signal(barrier, 1, device_id={"expert": (expert + k) % experts}, device_id_type=MESH)
        greeted += 1
    for k in range(1, ny):
        pl.semaphore_signal(barrier, 1, device_id={"dp": (y + k) % ny * nz + zl}, device_id_type=MESH)
        greeted += 1
    for k in range(1, nz):
        pl.semaphore_signal(barrier, 1, device_id={"dp": y * nz + (zl + k) % nz}, device_id_type=MESH)
        greeted += 1

    loads = [
        pltpu.make_async_copy(tok_hbm, tok_ref, load_sem.at[3]),
        pltpu.make_async_copy(wg_hbm, w_ref.at[:, pl.ds(0, half)], load_sem.at[0]),
        pltpu.make_async_copy(wu_hbm, w_ref.at[:, pl.ds(half, half)], load_sem.at[1]),
        pltpu.make_async_copy(hg_hbm, hg_ref, load_sem.at[2]),
    ]
    for load in loads:
        load.start()

    total = experts * slots
    row = lax.broadcasted_iota(jnp.int32, (total, tokens), 0)
    chosen = (ids_ref[0:1, :] == row // slots) | (ids_ref[1:2, :] == row // slots)
    earlier = lax.broadcasted_iota(jnp.int32, (tokens, tokens), 0) < lax.broadcasted_iota(
        jnp.int32, (tokens, tokens), 1
    )
    before = jnp.dot(
        jnp.where(chosen, 1.0, 0.0).astype(BF16),
        jnp.where(earlier, 1.0, 0.0).astype(BF16),
        preferred_element_type=F32,
    )
    table = jnp.where(chosen & (before == (row % slots).astype(F32)), 1.0, 0.0)
    table_ref[...] = table.T.astype(BF16)
    loads[0].wait()
    out_ref[...] = jnp.dot(table.astype(BF16), tok_ref[...], preferred_element_type=F32).astype(BF16)

    pl.semaphore_wait(barrier, greeted)

    def block(e):
        return pl.ds(pl.multiple_of(e * slots, slots), slots)

    sends = []
    dxs = [0, 2, 1, 3] if nx == 4 else [0]
    flat = 0
    for dx in dxs:
        for c in range(2):
            if dx == 0 and c == 1:
                continue
            other = 1 - core if dx == 0 else c
            to = ((x + nx - dx) % nx) * 2 + other
            slab = place(dx, core)
            src, dst = out_ref.at[block(to)], x_ref.at[block(slab)]
            if dx == 2:
                src, dst = out_ref.at[block(to), cols_of(y)], x_ref.at[block(slab), cols_of(y)]
            copy = remote(src, dst, a_send.at[flat], a_recv.at[slab], {"expert": to})
            copy.start()
            sends.append(copy)
            flat += 1
    x_ref[block(core), :] = out_ref[block(expert), :]

    def source(p):
        dx, c = slabs[p]
        return ((x + dx) % nx) * 2 + c

    def wait_slabs(j):
        for p in (2 * j, 2 * j + 1):
            if slabs[p][0] == 0:
                if p == 0:
                    q = 1 - core
                    remote(
                        out_ref.at[block(0)], x_ref.at[block(q)], a_send.at[0], a_recv.at[q], {"expert": expert}
                    ).wait_recv()
            elif slabs[p][0] != 2:
                remote(
                    out_ref.at[block(0)], x_ref.at[block(p)], a_send.at[0], a_recv.at[p], {"expert": expert}
                ).wait_recv()
            elif p % 2 == 0:
                for k in range(1, ny):
                    spread(k, y + ny - k).wait_recv()

    far_rows = pl.ds(2 * rows, rows)

    def spread(k, owner):
        ref = x_ref.at[far_rows, cols_of(owner % ny)]
        return remote(ref, ref, f_send.at[k - 1], f_recv.at[k - 1], {"dp": (y + k) % ny * nz + zl})

    def hand_on():
        for p in (4, 5):
            remote(
                out_ref.at[block(0), cols_of(y)],
                x_ref.at[block(p), cols_of(y)],
                a_send.at[0],
                a_recv.at[p],
                {"expert": expert},
            ).wait_recv()
        for k in range(1, ny):
            spread(k, y).start()
            sends.append(spread(k, y))

    def piece(j, d, h):
        return pl.ds(pl.multiple_of(j * rows + d * slots + h * part, part), part)

    lo, hi = pl.ds(0, half), pl.ds(half, half)

    def s1(j, d):
        return remote(s1_snd.at[j, d], s1_rcv.at[j, d], s1_send.at[j, d], s1_recv.at[j, d], pair[d])

    def s2(j, d):
        return remote(s2_snd.at[j, d], s2_rcv.at[j, d], s2_send.at[j, d], s2_recv.at[j, d], pair[1 - d])

    def g1(j, d, h):
        ref = d_ref.at[piece(j, d, h)]
        return remote(ref, ref, g1_send.at[j, d], g1_recv.at[j, d], pair[d])

    def stage0(j):
        wait_slabs(j)
        if j == 0:
            loads[1].wait()
            loads[2].wait()
        own = pl.ds(j * rows, rows)
        p_ref[own, :] = jnp.dot(x_ref[own, :], w_ref[...], preferred_element_type=F32)
        for d in range(2):
            s1_snd[j, d] = p_ref[piece(j, d, 1 - kept[d]), :].astype(BF16)
        for d in range(2):
            s1(j, d).start()
            sends.append(s1(j, d))

    def stage1(j):
        for d in range(2):
            mine = piece(j, d, kept[d])
            s1(j, d).wait_recv()
            both = p_ref[mine, :] + s1_rcv[j, d].astype(F32)
            p_ref[mine, :] = both
            s2_snd[j, d] = both.astype(BF16)
            s2(j, d).start()
            sends.append(s2(j, d))

    def stage2(j):
        if j == 0:
            loads[3].wait()
        for d in range(2):
            mine = piece(j, d, kept[d])
            hg_rows = pl.ds(pl.multiple_of(source(2 * j + d) * slots + kept[d] * part, part), part)
            upstream = hg_ref[hg_rows, :].astype(F32)
            s2(j, d).wait_recv()
            gate = p_ref[mine, lo] + s2_rcv[j, d, :, lo].astype(F32)
            upp = p_ref[mine, hi] + s2_rcv[j, d, :, hi].astype(F32)
            sg = jax.nn.sigmoid(gate)
            d_ref[mine, lo] = (upstream * upp * sg * (1.0 + gate * (1.0 - sg))).astype(BF16)
            d_ref[mine, hi] = (upstream * gate * sg).astype(BF16)
            g1(j, d, kept[d]).start()
            sends.append(g1(j, d, kept[d]))

    def stage4(j):
        for d in range(2):
            g1(j, d, 1 - kept[d]).wait_recv()
        own = pl.ds(j * rows, rows)
        rf_ref[own, :] = lax.dot_general(
            d_ref[own, :], w_ref[...], (((1,), (1,)), ((), ())), preferred_element_type=F32
        )
        r_ref[own, :] = rf_ref[own, :].astype(BF16)
        for k in range(1, ny):
            to = (y + k) % ny
            copy = remote(
                r_ref.at[own, cols_of(to)],
                yrcv.at[j, k - 1],
                y_send.at[j, k - 1],
                y_recv.at[j, k - 1],
                {"dp": to * nz + zl},
            )
            copy.start()
            sends.append(copy)

    def stage5(j):
        own = pl.ds(j * rows, rows)
        value = rf_ref[own, cols_of(y)]
        for k in range(1, ny):
            ref = yrcv.at[j, k - 1]
            remote(ref, ref, y_send.at[j, k - 1], y_recv.at[j, k - 1], {"dp": dp}).wait_recv()
            value = value + yrcv[j, k - 1].astype(F32)
        ysum[own, :] = value.astype(BF16)
        for p in (2 * j, 2 * j + 1):
            dx, c = slabs[p]
            if dx == 0:
                if p % 2:
                    continue
                p, to = 1 - core, x * 2 + 1 - core
            else:
                to = source(p)
            index = place((nx - dx) % nx, core)
            copy = remote(
                ysum.at[block(p)], ret_ref.at[block(expert)], r_send.at[p], r_recv.at[index], {"expert": to}
            )
            copy.start()
            sends.append(copy)
        if j == 0:
            ret_ref[block(expert), :] = ysum[block(core), :]

    if nx == 4:
        plan = (0, 0), (0, 1), "F", (0, 3), (1, 0), (0, 2), (1, 1), (1, 3), (1, 2), (2, 0), (2, 1), (2, 2), (2, 3), (4, 0), (4, 1), (4, 2), (5, 0), (5, 1), (4, 3), "V", (5, 2), (5, 3), "W"
    else:
        plan = (0, 0), (1, 0), (2, 0), (4, 0), "V", (5, 0), "W"
    step = min(256, width)
    early = width // step // 2

    def grads(i, carry):
        cols = pl.ds(pl.multiple_of(i * step, step), step)
        both = lax.dot_general(
            x_ref[:, cols], d_ref[...], (((0,), (0,)), ((), ())), preferred_element_type=F32
        ).astype(BF16)
        gg_ref[cols, :] = both[:, :half]
        ug_ref[cols, :] = both[:, half:]
        return carry

    stores = [
        pltpu.make_async_copy(gg_ref, gg_hbm, store_sem.at[0]),
        pltpu.make_async_copy(ug_ref, ug_hbm, store_sem.at[1]),
    ]
    stages = (stage0, stage1, stage2, None, stage4, stage5)
    for act in plan:
        if act == "F":
            hand_on()
        elif act == "V":
            lax.fori_loop(0, early, grads, 0)
        elif act == "W":
            lax.fori_loop(early, width // step, grads, 0)
            for store in stores:
                store.start()
        else:
            stages[act[0]](act[1])

    for p in range(len(slabs)):
        dx, c = slabs[p]
        if dx == 0:
            if p:
                continue
            index, e = 1 - core, x * 2 + 1 - core
        else:
            index, e = p, source(p)
        ref = ret_ref.at[block(e)]
        remote(ref, ref, r_send.at[0], r_recv.at[index], {"expert": expert}).wait_recv()
    sum_ref[...] = jnp.dot(table_ref[...], ret_ref[...], preferred_element_type=F32)
    zsnd[...] = sum_ref[...].astype(BF16)

    owners = z_send.shape[0]
    first = (nz - owners) // 2
    few = tokens // owners
    is_owner = (zl >= first) & (zl < first + owners)
    my_m = jnp.clip(zl - first, 0, owners - 1)

    def band(m):
        return pl.ds(pl.multiple_of(m * few, few), few)

    def z_out(q, m):
        rel = (zl + nz - (first + m)) % nz
        return remote(
            zsnd.at[band(m), pl.ds(q * span, span)],
            zrcv.at[rel, :, pl.ds(q * span, span)],
            z_send.at[m, q],
            z_recv.at[rel, q],
            {"dp": y * nz + first + m},
        )

    def h_out(q, k):
        ref = og_ref.at[band(my_m), cut_of(y, q)]
        return remote(ref, ref, h_send.at[k, q], h_recv.at[my_m, q], {"dp": y * nz + (zl + k) % nz})

    for q in range(cuts):
        for m in range(owners):
            pl.when(zl != first + m)(lambda q=q, m=m: z_out(q, m).start())

    @pl.when(is_owner)
    def _():
        for q in range(cuts):
            value = sum_ref[band(my_m), pl.ds(q * span, span)]
            for k in range(1, nz):
                ref = zrcv.at[k, :, pl.ds(q * span, span)]
                remote(ref, ref, z_send.at[0, q], z_recv.at[k, q], {"dp": dp}).wait_recv()
                value = value + zrcv[k, :, pl.ds(q * span, span)].astype(F32)
            og_ref[band(my_m), cut_of(y, q)] = value.astype(BF16)
            for k in range(1, nz):
                h_out(q, k).start()

    for q in range(cuts):
        for m in range(owners):

            @pl.when(zl != first + m)
            def _(q=q, m=m):
                ref = og_ref.at[band(m), cut_of(y, q)]
                remote(ref, ref, h_send.at[0, q], h_recv.at[m, q], {"dp": dp}).wait_recv()

        for k in range(1, ny):
            ref = og_ref.at[:, cut_of(y, q)]
            copy = remote(ref, ref, o_send.at[k - 1, q], o_recv.at[k - 1, q], {"dp": (y + k) % ny * nz + zl})
            copy.start()
            sends.append(copy)
    for q in range(cuts):
        for k in range(1, ny):
            ref = og_ref.at[:, cut_of((y + ny - k) % ny, q)]
            remote(ref, ref, o_send.at[k - 1, q], o_recv.at[k - 1, q], {"dp": dp}).wait_recv()
    tg_out[...] = og_ref[...]

    for copy in sends:
        copy.wait_send()
    for q in range(cuts):
        for m in range(owners):
            pl.when(zl != first + m)(lambda q=q, m=m: z_out(q, m).wait_send())

    @pl.when(is_owner)
    def _():
        for q in range(cuts):
            for k in range(1, nz):
                h_out(q, k).wait_send()

    for store in stores:
        store.wait()


def on_device(sizes, tokens, expert_ids, w_gate, w_up, hidden_grad):
    ny, nz, nx = sizes
    count, width = tokens.shape
    half = w_gate.shape[2]
    rows = hidden_grad.shape[1]
    chunks = nx
    part = rows // chunks // 4
    share = width // ny
    owners = min(4, nz)
    near = max(ny - 1, 1)
    cuts = 1
    scratch = [
        VMEM((count, width), BF16),
        VMEM((count, rows), BF16),
        VMEM((width, 2 * half), BF16),
        VMEM((rows, half), BF16),
        VMEM((rows, width), BF16),
        VMEM((rows, width), BF16),
        VMEM((rows, 2 * half), F32),
        VMEM((rows, 2 * half), BF16),
        VMEM((rows, width), BF16),
        VMEM((rows, width), F32),
        VMEM((chunks, near, rows // chunks, share), BF16),
        VMEM((rows, share), BF16),
        VMEM((rows, share), BF16),
        VMEM((chunks, 2, part, 2 * half), BF16),
        VMEM((chunks, 2, part, 2 * half), BF16),
        VMEM((chunks, 2, part, 2 * half), BF16),
        VMEM((chunks, 2, part, 2 * half), BF16),
        VMEM((count, share), F32),
        VMEM((count, share), BF16),
        VMEM((nz, count // owners, share), BF16),
        VMEM((count, width), BF16),
        VMEM((width, half), BF16),
        VMEM((width, half), BF16),
        DMA((4,)),
        DMA((2,)),
        DMA((2 * nx,)),
        DMA((2 * nx,)),
        DMA((near,)),
        DMA((near,)),
    ]
    scratch += [DMA((chunks, 2)) for _ in range(6)]
    scratch += [
        DMA((2 * nx,)),
        DMA((2 * nx,)),
        DMA((chunks, near)),
        DMA((chunks, near)),
        DMA((owners, cuts)),
        DMA((nz, cuts)),
        DMA((nz, cuts)),
        DMA((owners, cuts)),
        DMA((near, cuts)),
        DMA((near, cuts)),
    ]
    vmem = pl.BlockSpec(memory_space=VMEM)
    hbm = pl.BlockSpec(memory_space=pltpu.HBM)
    free = pl.BlockSpec(memory_space=ANY)
    tokens_grad, gate_grad, up_grad = pl.pallas_call(
        functools.partial(kernel, sizes),
        out_shape=(
            jax.ShapeDtypeStruct((count, width), BF16),
            jax.ShapeDtypeStruct((width, half), BF16),
            jax.ShapeDtypeStruct((width, half), BF16),
        ),
        in_specs=[vmem, hbm, hbm, hbm, hbm],
        out_specs=(vmem, free, free),
        scratch_shapes=scratch,
        compiler_params=pltpu.CompilerParams(
            collective_id=0, has_side_effects=True, vmem_limit_bytes=32 * 1024 * 1024
        ),
    )(
        expert_ids.T,
        pltpu.with_memory_space_constraint(tokens, pltpu.HBM),
        pltpu.with_memory_space_constraint(hidden_grad[0], pltpu.HBM),
        pltpu.with_memory_space_constraint(w_gate[0], pltpu.HBM),
        pltpu.with_memory_space_constraint(w_up[0], pltpu.HBM),
    )
    return tokens_grad, gate_grad[None], up_grad[None]


def solution(mesh):
    dp, experts = mesh.shape["dp"], mesh.shape["expert"]
    sizes = {32: (4, 8), 4: (2, 2), 2: (2, 1), 1: (1, 1)}[dp] + (experts // 2,)
    in_specs = (
        P("expert", "tensor"),
        P("expert", None),
        P("expert", "tensor", "dp"),
        P("expert", "tensor", "dp"),
        P("expert", None, "dp"),
    )
    out_specs = (P("expert", "tensor"), P("expert", "tensor", "dp"), P("expert", "tensor", "dp"))
    return jax.shard_map(
        functools.partial(on_device, sizes),
        mesh=mesh,
        in_specs=in_specs,
        out_specs=out_specs,
        check_vma=False,
    )
```

```python
import functools

import jax
import jax.numpy as jnp
from jax import lax
from jax.experimental import pallas as pl
from jax.experimental.pallas import tpu as pltpu
from jax.sharding import PartitionSpec as P

MESH = pl.DeviceIdType.MESH
F32, BF16 = jnp.float32, jnp.bfloat16
ANY = pl.ANY
VMEM = pltpu.VMEM
DMA = pltpu.SemaphoreType.DMA

SLABS = {
    4: ((0, 0), (0, 1), (1, 0), (3, 1), (2, 0), (2, 1), (1, 1), (3, 0)),
    1: ((0, 0), (0, 1)),
}


def remote(src, dst, send, recv, device):
    return pltpu.make_async_remote_copy(
        src_ref=src, dst_ref=dst, send_sem=send, recv_sem=recv, device_id=device, device_id_type=MESH
    )


def kernel(
    sizes,
    ids_ref,
    tok_hbm,
    hg_hbm,
    wg_hbm,
    wu_hbm,
    tg_out,
    gg_hbm,
    ug_hbm,
    tok_ref,
    table_ref,
    w_ref,
    hg_ref,
    out_ref,
    x_ref,
    p_ref,
    d_ref,
    r_ref,
    rf_ref,
    yrcv,
    ysum,
    ret_ref,
    s1_snd,
    s1_rcv,
    s2_snd,
    s2_rcv,
    sum_ref,
    zsnd,
    zrcv,
    og_ref,
    gg_ref,
    ug_ref,
    load_sem,
    store_sem,
    a_send,
    a_recv,
    f_send,
    f_recv,
    s1_send,
    s1_recv,
    s2_send,
    s2_recv,
    g1_send,
    g1_recv,
    r_send,
    r_recv,
    y_send,
    y_recv,
    z_send,
    z_recv,
    h_send,
    h_recv,
    o_send,
    o_recv,
):
    ny, nz, nx = sizes
    experts = 2 * nx
    tokens, width = tok_ref.shape
    slots = r_ref.shape[0] // experts
    half = w_ref.shape[1] // 2
    slabs = SLABS[nx]
    cuts = z_send.shape[1]
    share = width // ny
    span = share // cuts
    chunks = len(slabs) // 2
    rows = 2 * slots
    part = rows // 4

    expert = lax.axis_index("expert")
    core = expert % 2
    x = expert // 2
    dp = lax.axis_index("dp")
    y, zl = dp // nz, dp % nz
    zh = lax.axis_index("tensor")
    pair = ({"tensor": zh + 1 - 2 * (zh % 2)}, {"tensor": 3 - zh})
    kept = ((zh + 1) % 4 // 2, zh // 2)

    def place(dx, c):
        return {0: c, 1: 2 + 4 * c, 2: 4 + c, 3: 7 - 4 * c}[dx]

    def cols_of(k):
        return pl.ds(pl.multiple_of(k * share, 128), share)

    def cut_of(k, q):
        return pl.ds(pl.multiple_of(k * share + q * span, 128), span)

    barrier = pltpu.get_barrier_semaphore()
    greeted = 0
    for peer in pair:
        pl.semaphore_signal(barrier, 1, device_id=peer, device_id_type=MESH)
        greeted += 1
    for k in range(1, experts):
        pl.semaphore_signal(barrier, 1, device_id={"expert": (expert + k) % experts}, device_id_type=MESH)
        greeted += 1
    for k in range(1, ny):
        pl.semaphore_signal(barrier, 1, device_id={"dp": (y + k) % ny * nz + zl}, device_id_type=MESH)
        greeted += 1
    for k in range(1, nz):
        pl.semaphore_signal(barrier, 1, device_id={"dp": y * nz + (zl + k) % nz}, device_id_type=MESH)
        greeted += 1

    loads = [
        pltpu.make_async_copy(tok_hbm, tok_ref, load_sem.at[3]),
        pltpu.make_async_copy(wg_hbm, w_ref.at[:, pl.ds(0, half)], load_sem.at[0]),
        pltpu.make_async_copy(wu_hbm, w_ref.at[:, pl.ds(half, half)], load_sem.at[1]),
        pltpu.make_async_copy(hg_hbm, hg_ref, load_sem.at[2]),
    ]
    for load in loads:
        load.start()

    total = experts * slots
    row = lax.broadcasted_iota(jnp.int32, (total, tokens), 0)
    chosen = (ids_ref[0:1, :] == row // slots) | (ids_ref[1:2, :] == row // slots)
    earlier = lax.broadcasted_iota(jnp.int32, (tokens, tokens), 0) < lax.broadcasted_iota(
        jnp.int32, (tokens, tokens), 1
    )
    before = jnp.dot(
        jnp.where(chosen, 1.0, 0.0).astype(BF16),
        jnp.where(earlier, 1.0, 0.0).astype(BF16),
        preferred_element_type=F32,
    )
    table = jnp.where(chosen & (before == (row % slots).astype(F32)), 1.0, 0.0)
    table_ref[...] = table.T.astype(BF16)
    loads[0].wait()
    out_ref[...] = jnp.dot(table.astype(BF16), tok_ref[...], preferred_element_type=F32).astype(BF16)

    pl.semaphore_wait(barrier, greeted)

    def block(e):
        return pl.ds(pl.multiple_of(e * slots, slots), slots)

    sends = []
    flat = 0

    def send_slab(back, other, slab, share_only=False):
        nonlocal flat
        to = ((x + nx - back) % nx) * 2 + other
        src, dst = out_ref.at[block(to)], x_ref.at[block(slab)]
        if share_only:
            src, dst = out_ref.at[block(to), cols_of(y)], x_ref.at[block(slab), cols_of(y)]
        copy = remote(src, dst, a_send.at[flat], a_recv.at[slab], {"expert": to})
        copy.start()
        sends.append(copy)
        flat += 1

    send_slab(0, 1 - core, place(0, core))
    if nx == 4:
        for other in range(2):
            send_slab(1 + 2 * core, other, 2 + core)
        for other in range(2):
            send_slab(2, other, place(2, core), True)
        for other in range(2):
            send_slab(3 - 2 * core, other, 7 - core)
    x_ref[block(core), :] = out_ref[block(expert), :]

    def source(p):
        dx, c = slabs[p]
        return ((x + dx) % nx) * 2 + c

    def wait_slabs(j):
        for p in (2 * j, 2 * j + 1):
            if slabs[p][0] == 0:
                if p == 0:
                    q = 1 - core
                    remote(
                        out_ref.at[block(0)], x_ref.at[block(q)], a_send.at[0], a_recv.at[q], {"expert": expert}
                    ).wait_recv()
            elif slabs[p][0] != 2:
                remote(
                    out_ref.at[block(0)], x_ref.at[block(p)], a_send.at[0], a_recv.at[p], {"expert": expert}
                ).wait_recv()
            elif p % 2 == 0:
                for k in range(1, ny):
                    spread(k, y + ny - k).wait_recv()

    far_rows = pl.ds(2 * rows, rows)

    def spread(k, owner):
        ref = x_ref.at[far_rows, cols_of(owner % ny)]
        return remote(ref, ref, f_send.at[k - 1], f_recv.at[k - 1], {"dp": (y + k) % ny * nz + zl})

    def hand_on():
        for p in (4, 5):
            remote(
                out_ref.at[block(0), cols_of(y)],
                x_ref.at[block(p), cols_of(y)],
                a_send.at[0],
                a_recv.at[p],
                {"expert": expert},
            ).wait_recv()
        for k in range(1, ny):
            spread(k, y).start()
            sends.append(spread(k, y))

    def piece(j, d, h):
        return pl.ds(pl.multiple_of(j * rows + d * slots + h * part, part), part)

    lo, hi = pl.ds(0, half), pl.ds(half, half)

    def s1(j, d):
        return remote(s1_snd.at[j, d], s1_rcv.at[j, d], s1_send.at[j, d], s1_recv.at[j, d], pair[d])

    def s2(j, d):
        return remote(s2_snd.at[j, d], s2_rcv.at[j, d], s2_send.at[j, d], s2_recv.at[j, d], pair[1 - d])

    def g1(j, d, h):
        ref = d_ref.at[piece(j, d, h)]
        return remote(ref, ref, g1_send.at[j, d], g1_recv.at[j, d], pair[d])

    def stage0(j):
        wait_slabs(j)
        if j == 0:
            loads[1].wait()
            loads[2].wait()
        own = pl.ds(j * rows, rows)
        p_ref[own, :] = jnp.dot(x_ref[own, :], w_ref[...], preferred_element_type=F32)
        for d in range(2):
            s1_snd[j, d] = p_ref[piece(j, d, 1 - kept[d]), :].astype(BF16)
        for d in range(2):
            s1(j, d).start()
            sends.append(s1(j, d))

    def stage1(j):
        for d in range(2):
            mine = piece(j, d, kept[d])
            s1(j, d).wait_recv()
            both = p_ref[mine, :] + s1_rcv[j, d].astype(F32)
            p_ref[mine, :] = both
            s2_snd[j, d] = both.astype(BF16)
            s2(j, d).start()
            sends.append(s2(j, d))

    def stage2(j):
        if j == 0:
            loads[3].wait()
        for d in range(2):
            mine = piece(j, d, kept[d])
            hg_rows = pl.ds(pl.multiple_of(source(2 * j + d) * slots + kept[d] * part, part), part)
            upstream = hg_ref[hg_rows, :].astype(F32)
            s2(j, d).wait_recv()
            gate = p_ref[mine, lo] + s2_rcv[j, d, :, lo].astype(F32)
            upp = p_ref[mine, hi] + s2_rcv[j, d, :, hi].astype(F32)
            sg = jax.nn.sigmoid(gate)
            d_ref[mine, lo] = (upstream * upp * sg * (1.0 + gate * (1.0 - sg))).astype(BF16)
            d_ref[mine, hi] = (upstream * gate * sg).astype(BF16)
            g1(j, d, kept[d]).start()
            sends.append(g1(j, d, kept[d]))

    def stage4(j):
        for d in range(2):
            g1(j, d, 1 - kept[d]).wait_recv()
        own = pl.ds(j * rows, rows)
        rf_ref[own, :] = lax.dot_general(
            d_ref[own, :], w_ref[...], (((1,), (1,)), ((), ())), preferred_element_type=F32
        )
        r_ref[own, :] = rf_ref[own, :].astype(BF16)
        for k in range(1, ny):
            to = (y + k) % ny
            copy = remote(
                r_ref.at[own, cols_of(to)],
                yrcv.at[j, k - 1],
                y_send.at[j, k - 1],
                y_recv.at[j, k - 1],
                {"dp": to * nz + zl},
            )
            copy.start()
            sends.append(copy)

    def stage5(j):
        own = pl.ds(j * rows, rows)
        value = rf_ref[own, cols_of(y)]
        for k in range(1, ny):
            ref = yrcv.at[j, k - 1]
            remote(ref, ref, y_send.at[j, k - 1], y_recv.at[j, k - 1], {"dp": dp}).wait_recv()
            value = value + yrcv[j, k - 1].astype(F32)
        ysum[own, :] = value.astype(BF16)
        for p in (2 * j, 2 * j + 1):
            dx, c = slabs[p]
            if dx == 0:
                if p % 2:
                    continue
                p, to = 1 - core, x * 2 + 1 - core
            else:
                to = source(p)
            index = place((nx - dx) % nx, core)
            copy = remote(
                ysum.at[block(p)], ret_ref.at[block(expert)], r_send.at[p], r_recv.at[index], {"expert": to}
            )
            copy.start()
            sends.append(copy)
        if j == 0:
            ret_ref[block(expert), :] = ysum[block(core), :]

    if nx == 4:
        plan = (0, 0), (0, 1), "F", (0, 3), (1, 0), (0, 2), (1, 1), (1, 3), (1, 2), (2, 0), (2, 1), (2, 2), (2, 3), (4, 0), (4, 1), (4, 2), (5, 0), (5, 1), (4, 3), "V", (5, 2), (5, 3), "W"
    else:
        plan = (0, 0), (1, 0), (2, 0), (4, 0), "V", (5, 0), "W"
    step = min(256, width)
    early = width // step // 2

    def grads(i, carry):
        cols = pl.ds(pl.multiple_of(i * step, step), step)
        both = lax.dot_general(
            x_ref[:, cols], d_ref[...], (((0,), (0,)), ((), ())), preferred_element_type=F32
        ).astype(BF16)
        gg_ref[cols, :] = both[:, :half]
        ug_ref[cols, :] = both[:, half:]
        return carry

    stores = [
        pltpu.make_async_copy(gg_ref, gg_hbm, store_sem.at[0]),
        pltpu.make_async_copy(ug_ref, ug_hbm, store_sem.at[1]),
    ]
    stages = (stage0, stage1, stage2, None, stage4, stage5)
    for act in plan:
        if act == "F":
            hand_on()
        elif act == "V":
            lax.fori_loop(0, early, grads, 0)
        elif act == "W":
            lax.fori_loop(early, width // step, grads, 0)
            for store in stores:
                store.start()
        else:
            stages[act[0]](act[1])

    for p in range(len(slabs)):
        dx, c = slabs[p]
        if dx == 0:
            if p:
                continue
            index, e = 1 - core, x * 2 + 1 - core
        else:
            index, e = p, source(p)
        ref = ret_ref.at[block(e)]
        remote(ref, ref, r_send.at[0], r_recv.at[index], {"expert": expert}).wait_recv()
    sum_ref[...] = jnp.dot(table_ref[...], ret_ref[...], preferred_element_type=F32)
    zsnd[...] = sum_ref[...].astype(BF16)

    owners = z_send.shape[0]
    first = (nz - owners) // 2
    few = tokens // owners
    is_owner = (zl >= first) & (zl < first + owners)
    my_m = jnp.clip(zl - first, 0, owners - 1)

    def band(m):
        return pl.ds(pl.multiple_of(m * few, few), few)

    def z_out(q, m):
        rel = (zl + nz - (first + m)) % nz
        return remote(
            zsnd.at[band(m), pl.ds(q * span, span)],
            zrcv.at[rel, :, pl.ds(q * span, span)],
            z_send.at[m, q],
            z_recv.at[rel, q],
            {"dp": y * nz + first + m},
        )

    def h_out(q, k):
        ref = og_ref.at[band(my_m), cut_of(y, q)]
        return remote(ref, ref, h_send.at[k, q], h_recv.at[my_m, q], {"dp": y * nz + (zl + k) % nz})

    for q in range(cuts):
        for m in range(owners):
            pl.when(zl != first + m)(lambda q=q, m=m: z_out(q, m).start())

    @pl.when(is_owner)
    def _():
        for q in range(cuts):
            value = sum_ref[band(my_m), pl.ds(q * span, span)]
            for k in range(1, nz):
                ref = zrcv.at[k, :, pl.ds(q * span, span)]
                remote(ref, ref, z_send.at[0, q], z_recv.at[k, q], {"dp": dp}).wait_recv()
                value = value + zrcv[k, :, pl.ds(q * span, span)].astype(F32)
            og_ref[band(my_m), cut_of(y, q)] = value.astype(BF16)
            for k in range(1, nz):
                h_out(q, k).start()

    for q in range(cuts):
        for m in range(owners):

            @pl.when(zl != first + m)
            def _(q=q, m=m):
                ref = og_ref.at[band(m), cut_of(y, q)]
                remote(ref, ref, h_send.at[0, q], h_recv.at[m, q], {"dp": dp}).wait_recv()

        for k in range(1, ny):
            ref = og_ref.at[:, cut_of(y, q)]
            copy = remote(ref, ref, o_send.at[k - 1, q], o_recv.at[k - 1, q], {"dp": (y + k) % ny * nz + zl})
            copy.start()
            sends.append(copy)
    for q in range(cuts):
        for k in range(1, ny):
            ref = og_ref.at[:, cut_of((y + ny - k) % ny, q)]
            remote(ref, ref, o_send.at[k - 1, q], o_recv.at[k - 1, q], {"dp": dp}).wait_recv()
    tg_out[...] = og_ref[...]

    for copy in sends:
        copy.wait_send()
    for q in range(cuts):
        for m in range(owners):
            pl.when(zl != first + m)(lambda q=q, m=m: z_out(q, m).wait_send())

    @pl.when(is_owner)
    def _():
        for q in range(cuts):
            for k in range(1, nz):
                h_out(q, k).wait_send()

    for store in stores:
        store.wait()


def on_device(sizes, tokens, expert_ids, w_gate, w_up, hidden_grad):
    ny, nz, nx = sizes
    count, width = tokens.shape
    half = w_gate.shape[2]
    rows = hidden_grad.shape[1]
    chunks = nx
    part = rows // chunks // 4
    share = width // ny
    owners = min(2, nz)
    near = max(ny - 1, 1)
    cuts = 1
    scratch = [
        VMEM((count, width), BF16),
        VMEM((count, rows), BF16),
        VMEM((width, 2 * half), BF16),
        VMEM((rows, half), BF16),
        VMEM((rows, width), BF16),
        VMEM((rows, width), BF16),
        VMEM((rows, 2 * half), F32),
        VMEM((rows, 2 * half), BF16),
        VMEM((rows, width), BF16),
        VMEM((rows, width), F32),
        VMEM((chunks, near, rows // chunks, share), BF16),
        VMEM((rows, share), BF16),
        VMEM((rows, share), BF16),
        VMEM((chunks, 2, part, 2 * half), BF16),
        VMEM((chunks, 2, part, 2 * half), BF16),
        VMEM((chunks, 2, part, 2 * half), BF16),
        VMEM((chunks, 2, part, 2 * half), BF16),
        VMEM((count, share), F32),
        VMEM((count, share), BF16),
        VMEM((nz, count // owners, share), BF16),
        VMEM((count, width), BF16),
        VMEM((width, half), BF16),
        VMEM((width, half), BF16),
        DMA((4,)),
        DMA((2,)),
        DMA((2 * nx,)),
        DMA((2 * nx,)),
        DMA((near,)),
        DMA((near,)),
    ]
    scratch += [DMA((chunks, 2)) for _ in range(6)]
    scratch += [
        DMA((2 * nx,)),
        DMA((2 * nx,)),
        DMA((chunks, near)),
        DMA((chunks, near)),
        DMA((owners, cuts)),
        DMA((nz, cuts)),
        DMA((nz, cuts)),
        DMA((owners, cuts)),
        DMA((near, cuts)),
        DMA((near, cuts)),
    ]
    vmem = pl.BlockSpec(memory_space=VMEM)
    hbm = pl.BlockSpec(memory_space=pltpu.HBM)
    free = pl.BlockSpec(memory_space=ANY)
    tokens_grad, gate_grad, up_grad = pl.pallas_call(
        functools.partial(kernel, sizes),
        out_shape=(
            jax.ShapeDtypeStruct((count, width), BF16),
            jax.ShapeDtypeStruct((width, half), BF16),
            jax.ShapeDtypeStruct((width, half), BF16),
        ),
        in_specs=[vmem, hbm, hbm, hbm, hbm],
        out_specs=(vmem, free, free),
        scratch_shapes=scratch,
        compiler_params=pltpu.CompilerParams(
            collective_id=0, has_side_effects=True, vmem_limit_bytes=32 * 1024 * 1024
        ),
    )(
        expert_ids.T,
        pltpu.with_memory_space_constraint(tokens, pltpu.HBM),
        pltpu.with_memory_space_constraint(hidden_grad[0], pltpu.HBM),
        pltpu.with_memory_space_constraint(w_gate[0], pltpu.HBM),
        pltpu.with_memory_space_constraint(w_up[0], pltpu.HBM),
    )
    return tokens_grad, gate_grad[None], up_grad[None]


def solution(mesh):
    dp, experts = mesh.shape["dp"], mesh.shape["expert"]
    sizes = {32: (4, 8), 4: (2, 2), 2: (2, 1), 1: (1, 1)}[dp] + (experts // 2,)
    in_specs = (
        P("expert", "tensor"),
        P("expert", None),
        P("expert", "tensor", "dp"),
        P("expert", "tensor", "dp"),
        P("expert", None, "dp"),
    )
    out_specs = (P("expert", "tensor"), P("expert", "tensor", "dp"), P("expert", "tensor", "dp"))
    return jax.shard_map(
        functools.partial(on_device, sizes),
        mesh=mesh,
        in_specs=in_specs,
        out_specs=out_specs,
        check_vma=False,
    )
```

```python
import functools

import jax
import jax.numpy as jnp
from jax import lax
from jax.experimental import pallas as pl
from jax.experimental.pallas import tpu as pltpu
from jax.sharding import PartitionSpec as P

MESH = pl.DeviceIdType.MESH
F32, BF16 = jnp.float32, jnp.bfloat16
ANY = pl.ANY
VMEM = pltpu.VMEM
DMA = pltpu.SemaphoreType.DMA

SLABS = {
    4: ((0, 0), (0, 1), (1, 0), (3, 1), (2, 0), (2, 1), (1, 1), (3, 0)),
    1: ((0, 0), (0, 1)),
}


def remote(src, dst, send, recv, device):
    return pltpu.make_async_remote_copy(
        src_ref=src, dst_ref=dst, send_sem=send, recv_sem=recv, device_id=device, device_id_type=MESH
    )


def kernel(
    sizes,
    ids_ref,
    tok_hbm,
    hg_hbm,
    wg_hbm,
    wu_hbm,
    tg_out,
    gg_hbm,
    ug_hbm,
    tok_ref,
    table_ref,
    w_ref,
    hg_ref,
    out_ref,
    x_ref,
    p_ref,
    d_ref,
    r_ref,
    rf_ref,
    yrcv,
    ysum,
    ret_ref,
    s1_snd,
    s1_rcv,
    s2_snd,
    s2_rcv,
    sum_ref,
    zsnd,
    zrcv,
    og_ref,
    gg_ref,
    ug_ref,
    load_sem,
    store_sem,
    a_send,
    a_recv,
    f_send,
    f_recv,
    s1_send,
    s1_recv,
    s2_send,
    s2_recv,
    g1_send,
    g1_recv,
    r_send,
    r_recv,
    y_send,
    y_recv,
    z_send,
    z_recv,
    h_send,
    h_recv,
    o_send,
    o_recv,
):
    ny, nz, nx = sizes
    experts = 2 * nx
    tokens, width = tok_ref.shape
    slots = r_ref.shape[0] // experts
    half = w_ref.shape[1] // 2
    slabs = SLABS[nx]
    cuts = z_send.shape[1]
    share = width // ny
    span = share // cuts
    chunks = len(slabs) // 2
    rows = 2 * slots
    part = rows // 4

    expert = lax.axis_index("expert")
    core = expert % 2
    x = expert // 2
    dp = lax.axis_index("dp")
    y, zl = dp // nz, dp % nz
    zh = lax.axis_index("tensor")
    pair = ({"tensor": zh + 1 - 2 * (zh % 2)}, {"tensor": 3 - zh})
    kept = ((zh + 1) % 4 // 2, zh // 2)

    def place(dx, c):
        return {0: c, 1: 2 + 4 * c, 2: 4 + c, 3: 7 - 4 * c}[dx]

    def cols_of(k):
        return pl.ds(pl.multiple_of(k * share, 128), share)

    def cut_of(k, q):
        return pl.ds(pl.multiple_of(k * share + q * span, 128), span)

    barrier = pltpu.get_barrier_semaphore()
    greeted = 0
    for peer in pair:
        pl.semaphore_signal(barrier, 1, device_id=peer, device_id_type=MESH)
        greeted += 1
    for k in range(1, experts):
        pl.semaphore_signal(barrier, 1, device_id={"expert": (expert + k) % experts}, device_id_type=MESH)
        greeted += 1
    for k in range(1, ny):
        pl.semaphore_signal(barrier, 1, device_id={"dp": (y + k) % ny * nz + zl}, device_id_type=MESH)
        greeted += 1
    for k in range(1, nz):
        pl.semaphore_signal(barrier, 1, device_id={"dp": y * nz + (zl + k) % nz}, device_id_type=MESH)
        greeted += 1

    loads = [
        pltpu.make_async_copy(tok_hbm, tok_ref, load_sem.at[3]),
        pltpu.make_async_copy(wg_hbm, w_ref.at[:, pl.ds(0, half)], load_sem.at[0]),
        pltpu.make_async_copy(wu_hbm, w_ref.at[:, pl.ds(half, half)], load_sem.at[1]),
        pltpu.make_async_copy(hg_hbm, hg_ref, load_sem.at[2]),
    ]
    for load in loads:
        load.start()

    total = experts * slots
    row = lax.broadcasted_iota(jnp.int32, (total, tokens), 0)
    chosen = (ids_ref[0:1, :] == row // slots) | (ids_ref[1:2, :] == row // slots)
    earlier = lax.broadcasted_iota(jnp.int32, (tokens, tokens), 0) < lax.broadcasted_iota(
        jnp.int32, (tokens, tokens), 1
    )
    before = jnp.dot(
        jnp.where(chosen, 1.0, 0.0).astype(BF16),
        jnp.where(earlier, 1.0, 0.0).astype(BF16),
        preferred_element_type=F32,
    )
    table = jnp.where(chosen & (before == (row % slots).astype(F32)), 1.0, 0.0)
    table_ref[...] = table.T.astype(BF16)
    loads[0].wait()
    out_ref[...] = jnp.dot(table.astype(BF16), tok_ref[...], preferred_element_type=F32).astype(BF16)

    pl.semaphore_wait(barrier, greeted)

    def block(e):
        return pl.ds(pl.multiple_of(e * slots, slots), slots)

    sends = []
    flat = 0

    def send_slab(back, other, slab, share_only=False):
        nonlocal flat
        to = ((x + nx - back) % nx) * 2 + other
        src, dst = out_ref.at[block(to)], x_ref.at[block(slab)]
        if share_only:
            src, dst = out_ref.at[block(to), cols_of(y)], x_ref.at[block(slab), cols_of(y)]
        copy = remote(src, dst, a_send.at[flat], a_recv.at[slab], {"expert": to})
        copy.start()
        sends.append(copy)
        flat += 1

    send_slab(0, 1 - core, place(0, core))
    if nx == 4:
        for other in range(2):
            send_slab(1 + 2 * core, other, 2 + core)
        for other in range(2):
            send_slab(2, other, place(2, core), True)
        for other in range(2):
            send_slab(3 - 2 * core, other, 7 - core)
    x_ref[block(core), :] = out_ref[block(expert), :]

    def source(p):
        dx, c = slabs[p]
        return ((x + dx) % nx) * 2 + c

    def wait_slabs(j):
        for p in (2 * j, 2 * j + 1):
            if slabs[p][0] == 0:
                if p == 0:
                    q = 1 - core
                    remote(
                        out_ref.at[block(0)], x_ref.at[block(q)], a_send.at[0], a_recv.at[q], {"expert": expert}
                    ).wait_recv()
            elif slabs[p][0] != 2:
                remote(
                    out_ref.at[block(0)], x_ref.at[block(p)], a_send.at[0], a_recv.at[p], {"expert": expert}
                ).wait_recv()
            elif p % 2 == 0:
                for k in range(1, ny):
                    spread(k, y + ny - k).wait_recv()

    far_rows = pl.ds(2 * rows, rows)

    def spread(k, owner):
        ref = x_ref.at[far_rows, cols_of(owner % ny)]
        return remote(ref, ref, f_send.at[k - 1], f_recv.at[k - 1], {"dp": (y + k) % ny * nz + zl})

    def hand_on():
        for p in (4, 5):
            remote(
                out_ref.at[block(0), cols_of(y)],
                x_ref.at[block(p), cols_of(y)],
                a_send.at[0],
                a_recv.at[p],
                {"expert": expert},
            ).wait_recv()
        for k in range(1, ny):
            spread(k, y).start()
            sends.append(spread(k, y))

    def piece(j, d, h):
        return pl.ds(pl.multiple_of(j * rows + d * slots + h * part, part), part)

    lo, hi = pl.ds(0, half), pl.ds(half, half)

    def s1(j, d):
        return remote(s1_snd.at[j, d], s1_rcv.at[j, d], s1_send.at[j, d], s1_recv.at[j, d], pair[d])

    def s2(j, d):
        return remote(s2_snd.at[j, d], s2_rcv.at[j, d], s2_send.at[j, d], s2_recv.at[j, d], pair[1 - d])

    def g1(j, d, h):
        ref = d_ref.at[piece(j, d, h)]
        return remote(ref, ref, g1_send.at[j, d], g1_recv.at[j, d], pair[d])

    def stage0(j):
        wait_slabs(j)
        if j == 0:
            loads[1].wait()
            loads[2].wait()
        own = pl.ds(j * rows, rows)
        p_ref[own, :] = jnp.dot(x_ref[own, :], w_ref[...], preferred_element_type=F32)
        for d in range(2):
            s1_snd[j, d] = p_ref[piece(j, d, 1 - kept[d]), :].astype(BF16)
        for d in range(2):
            s1(j, d).start()
            sends.append(s1(j, d))

    def stage1(j):
        for d in range(2):
            mine = piece(j, d, kept[d])
            s1(j, d).wait_recv()
            both = p_ref[mine, :] + s1_rcv[j, d].astype(F32)
            p_ref[mine, :] = both
            s2_snd[j, d] = both.astype(BF16)
            s2(j, d).start()
            sends.append(s2(j, d))

    def stage2(j):
        if j == 0:
            loads[3].wait()
        for d in range(2):
            mine = piece(j, d, kept[d])
            hg_rows = pl.ds(pl.multiple_of(source(2 * j + d) * slots + kept[d] * part, part), part)
            upstream = hg_ref[hg_rows, :].astype(F32)
            s2(j, d).wait_recv()
            gate = p_ref[mine, lo] + s2_rcv[j, d, :, lo].astype(F32)
            upp = p_ref[mine, hi] + s2_rcv[j, d, :, hi].astype(F32)
            sg = jax.nn.sigmoid(gate)
            d_ref[mine, lo] = (upstream * upp * sg * (1.0 + gate * (1.0 - sg))).astype(BF16)
            d_ref[mine, hi] = (upstream * gate * sg).astype(BF16)
            g1(j, d, kept[d]).start()
            sends.append(g1(j, d, kept[d]))

    def stage4(j):
        for d in range(2):
            g1(j, d, 1 - kept[d]).wait_recv()
        own = pl.ds(j * rows, rows)
        rf_ref[own, :] = lax.dot_general(
            d_ref[own, :], w_ref[...], (((1,), (1,)), ((), ())), preferred_element_type=F32
        )
        r_ref[own, :] = rf_ref[own, :].astype(BF16)
        for k in range(1, ny):
            to = (y + k) % ny
            copy = remote(
                r_ref.at[own, cols_of(to)],
                yrcv.at[j, k - 1],
                y_send.at[j, k - 1],
                y_recv.at[j, k - 1],
                {"dp": to * nz + zl},
            )
            copy.start()
            sends.append(copy)

    def stage5(j):
        own = pl.ds(j * rows, rows)
        value = rf_ref[own, cols_of(y)]
        for k in range(1, ny):
            ref = yrcv.at[j, k - 1]
            remote(ref, ref, y_send.at[j, k - 1], y_recv.at[j, k - 1], {"dp": dp}).wait_recv()
            value = value + yrcv[j, k - 1].astype(F32)
        ysum[own, :] = value.astype(BF16)
        for p in (2 * j, 2 * j + 1):
            dx, c = slabs[p]
            if dx == 0:
                if p % 2:
                    continue
                p, to = 1 - core, x * 2 + 1 - core
            else:
                to = source(p)
            index = place((nx - dx) % nx, core)
            copy = remote(
                ysum.at[block(p)], ret_ref.at[block(expert)], r_send.at[p], r_recv.at[index], {"expert": to}
            )
            copy.start()
            sends.append(copy)
        if j == 0:
            ret_ref[block(expert), :] = ysum[block(core), :]

    if nx == 4:
        plan = (0, 0), (0, 1), "F", (0, 3), (1, 0), (0, 2), (1, 1), (1, 3), (1, 2), (2, 0), (2, 1), (2, 2), (2, 3), (4, 0), (4, 1), (4, 2), (5, 0), (5, 1), (4, 3), (5, 2), "V", (5, 3), "W"
    else:
        plan = (0, 0), (1, 0), (2, 0), (4, 0), "V", (5, 0), "W"
    step = min(256, width)
    early = width // step // 2

    def grads(i, carry):
        cols = pl.ds(pl.multiple_of(i * step, step), step)
        both = lax.dot_general(
            x_ref[:, cols], d_ref[...], (((0,), (0,)), ((), ())), preferred_element_type=F32
        ).astype(BF16)
        gg_ref[cols, :] = both[:, :half]
        ug_ref[cols, :] = both[:, half:]
        return carry

    stores = [
        pltpu.make_async_copy(gg_ref, gg_hbm, store_sem.at[0]),
        pltpu.make_async_copy(ug_ref, ug_hbm, store_sem.at[1]),
    ]
    stages = (stage0, stage1, stage2, None, stage4, stage5)
    for act in plan:
        if act == "F":
            hand_on()
        elif act == "V":
            lax.fori_loop(0, early, grads, 0)
        elif act == "W":
            lax.fori_loop(early, width // step, grads, 0)
            for store in stores:
                store.start()
        else:
            stages[act[0]](act[1])

    for p in range(len(slabs)):
        dx, c = slabs[p]
        if dx == 0:
            if p:
                continue
            index, e = 1 - core, x * 2 + 1 - core
        else:
            index, e = p, source(p)
        ref = ret_ref.at[block(e)]
        remote(ref, ref, r_send.at[0], r_recv.at[index], {"expert": expert}).wait_recv()
    sum_ref[...] = jnp.dot(table_ref[...], ret_ref[...], preferred_element_type=F32)
    zsnd[...] = sum_ref[...].astype(BF16)

    owners = z_send.shape[0]
    first = (nz - owners) // 2
    few = tokens // owners
    is_owner = (zl >= first) & (zl < first + owners)
    my_m = jnp.clip(zl - first, 0, owners - 1)

    def band(m):
        return pl.ds(pl.multiple_of(m * few, few), few)

    def z_out(q, m):
        rel = (zl + nz - (first + m)) % nz
        return remote(
            zsnd.at[band(m), pl.ds(q * span, span)],
            zrcv.at[rel, :, pl.ds(q * span, span)],
            z_send.at[m, q],
            z_recv.at[rel, q],
            {"dp": y * nz + first + m},
        )

    def h_out(q, k):
        ref = og_ref.at[band(my_m), cut_of(y, q)]
        return remote(ref, ref, h_send.at[k, q], h_recv.at[my_m, q], {"dp": y * nz + (zl + k) % nz})

    for q in range(cuts):
        for m in range(owners):
            pl.when(zl != first + m)(lambda q=q, m=m: z_out(q, m).start())

    @pl.when(is_owner)
    def _():
        for q in range(cuts):
            value = sum_ref[band(my_m), pl.ds(q * span, span)]
            for k in range(1, nz):
                ref = zrcv.at[k, :, pl.ds(q * span, span)]
                remote(ref, ref, z_send.at[0, q], z_recv.at[k, q], {"dp": dp}).wait_recv()
                value = value + zrcv[k, :, pl.ds(q * span, span)].astype(F32)
            og_ref[band(my_m), cut_of(y, q)] = value.astype(BF16)
            for k in range(1, nz):
                h_out(q, k).start()

    for q in range(cuts):
        for m in range(owners):

            @pl.when(zl != first + m)
            def _(q=q, m=m):
                ref = og_ref.at[band(m), cut_of(y, q)]
                remote(ref, ref, h_send.at[0, q], h_recv.at[m, q], {"dp": dp}).wait_recv()

        for k in range(1, ny):
            ref = og_ref.at[:, cut_of(y, q)]
            copy = remote(ref, ref, o_send.at[k - 1, q], o_recv.at[k - 1, q], {"dp": (y + k) % ny * nz + zl})
            copy.start()
            sends.append(copy)
    for q in range(cuts):
        for k in range(1, ny):
            ref = og_ref.at[:, cut_of((y + ny - k) % ny, q)]
            remote(ref, ref, o_send.at[k - 1, q], o_recv.at[k - 1, q], {"dp": dp}).wait_recv()
    tg_out[...] = og_ref[...]

    for copy in sends:
        copy.wait_send()
    for q in range(cuts):
        for m in range(owners):
            pl.when(zl != first + m)(lambda q=q, m=m: z_out(q, m).wait_send())

    @pl.when(is_owner)
    def _():
        for q in range(cuts):
            for k in range(1, nz):
                h_out(q, k).wait_send()

    for store in stores:
        store.wait()


def on_device(sizes, tokens, expert_ids, w_gate, w_up, hidden_grad):
    ny, nz, nx = sizes
    count, width = tokens.shape
    half = w_gate.shape[2]
    rows = hidden_grad.shape[1]
    chunks = nx
    part = rows // chunks // 4
    share = width // ny
    owners = min(2, nz)
    near = max(ny - 1, 1)
    cuts = 1
    scratch = [
        VMEM((count, width), BF16),
        VMEM((count, rows), BF16),
        VMEM((width, 2 * half), BF16),
        VMEM((rows, half), BF16),
        VMEM((rows, width), BF16),
        VMEM((rows, width), BF16),
        VMEM((rows, 2 * half), F32),
        VMEM((rows, 2 * half), BF16),
        VMEM((rows, width), BF16),
        VMEM((rows, width), F32),
        VMEM((chunks, near, rows // chunks, share), BF16),
        VMEM((rows, share), BF16),
        VMEM((rows, share), BF16),
        VMEM((chunks, 2, part, 2 * half), BF16),
        VMEM((chunks, 2, part, 2 * half), BF16),
        VMEM((chunks, 2, part, 2 * half), BF16),
        VMEM((chunks, 2, part, 2 * half), BF16),
        VMEM((count, share), F32),
        VMEM((count, share), BF16),
        VMEM((nz, count // owners, share), BF16),
        VMEM((count, width), BF16),
        VMEM((width, half), BF16),
        VMEM((width, half), BF16),
        DMA((4,)),
        DMA((2,)),
        DMA((2 * nx,)),
        DMA((2 * nx,)),
        DMA((near,)),
        DMA((near,)),
    ]
    scratch += [DMA((chunks, 2)) for _ in range(6)]
    scratch += [
        DMA((2 * nx,)),
        DMA((2 * nx,)),
        DMA((chunks, near)),
        DMA((chunks, near)),
        DMA((owners, cuts)),
        DMA((nz, cuts)),
        DMA((nz, cuts)),
        DMA((owners, cuts)),
        DMA((near, cuts)),
        DMA((near, cuts)),
    ]
    vmem = pl.BlockSpec(memory_space=VMEM)
    hbm = pl.BlockSpec(memory_space=pltpu.HBM)
    free = pl.BlockSpec(memory_space=ANY)
    tokens_grad, gate_grad, up_grad = pl.pallas_call(
        functools.partial(kernel, sizes),
        out_shape=(
            jax.ShapeDtypeStruct((count, width), BF16),
            jax.ShapeDtypeStruct((width, half), BF16),
            jax.ShapeDtypeStruct((width, half), BF16),
        ),
        in_specs=[vmem, hbm, hbm, hbm, hbm],
        out_specs=(vmem, free, free),
        scratch_shapes=scratch,
        compiler_params=pltpu.CompilerParams(
            collective_id=0, has_side_effects=True, vmem_limit_bytes=32 * 1024 * 1024
        ),
    )(
        expert_ids.T,
        pltpu.with_memory_space_constraint(tokens, pltpu.HBM),
        pltpu.with_memory_space_constraint(hidden_grad[0], pltpu.HBM),
        pltpu.with_memory_space_constraint(w_gate[0], pltpu.HBM),
        pltpu.with_memory_space_constraint(w_up[0], pltpu.HBM),
    )
    return tokens_grad, gate_grad[None], up_grad[None]


def solution(mesh):
    dp, experts = mesh.shape["dp"], mesh.shape["expert"]
    sizes = {32: (4, 8), 4: (2, 2), 2: (2, 1), 1: (1, 1)}[dp] + (experts // 2,)
    in_specs = (
        P("expert", "tensor"),
        P("expert", None),
        P("expert", "tensor", "dp"),
        P("expert", "tensor", "dp"),
        P("expert", None, "dp"),
    )
    out_specs = (P("expert", "tensor"), P("expert", "tensor", "dp"), P("expert", "tensor", "dp"))
    return jax.shard_map(
        functools.partial(on_device, sizes),
        mesh=mesh,
        in_specs=in_specs,
        out_specs=out_specs,
        check_vma=False,
    )
```
